128 devices in a mesh: outer: 4 (over z), inner: 32 (over y, x, core).
Axes of the slice: x: 4, y: 4, z: 4, core: 2. Of those that a mesh axis runs over, the one named last changes fastest.
Arguments:
- points: bfloat16 [64, 1048576], P(None, ('outer', 'inner')), may hold values from -6 to 6, as said below
- tree_order: int32 [1048576], P(('outer', 'inner')), may hold values from 0 to 8191, as said below
- rhs: float32 [32, 1048576], P(None, ('outer', 'inner')), may hold values from -6 to 6
- leaf_skel: int32 [2048, 256], P(('outer', 'inner')), may hold values from 0 to 511, as said below
- skel_mid: int32 [512, 256], P(('outer', 'inner')), may hold values from 0 to 1023, as said below
- skel_top: int32 [128, 256], replicated, may hold values from 0 to 1023, as said below
- near_lists: int32 [2048, 4], P(('outer', 'inner')), may hold values from 0 to 2047, as said below
- far_mid: int32 [512, 4], P(('outer', 'inner')), may hold values from 0 to 511, as said below
- far_top: int32 [128, 4], replicated, may hold values from 0 to 127, as said below
- leaf_interp: bfloat16 [2048, 256, 512], P(('outer', 'inner')), may hold values from -0.25 to 0.25
- interp_mid: bfloat16 [512, 256, 1024], P(('outer', 'inner')), may hold values from -0.1875 to 0.1875
- interp_top: bfloat16 [512, 256, 256], P(('outer', 'inner')), may hold values from -0.1875 to 0.1875
Outputs:
- solution: float32 [32, 1048576], P(None, ('outer', 'inner'))
- residual: float32 [32, 1048576], P(None, ('outer', 'inner'))
The draws below stay inside these ranges and needn't reach their ends.
Inputs may be any that keep to these rules, and one draw needn't show every extreme that they name: `points`: random values with no further structure. `tree_order`: each aligned block of 8192 entries is a permutation of 0 to 8191. `leaf_skel`: the entries of a row are distinct. `skel_mid`: the entries of a row are distinct. `skel_top`: the entries of a row are distinct. `near_lists`: each aligned block of 16 leaves splits into four groups of four leaves; a leaf's row lists its group, itself first. `far_mid`: each aligned block of 16 nodes splits into four groups of four nodes; a node's row lists its group, itself first. `far_top`: each aligned block of 16 nodes splits into four groups of four nodes; a node's row lists its group, itself first.
All inputs are finite; a program needn't handle non-finite values.
Results may differ from the reference program's by a relative error of at most 0.029.
Values may be sent and summed in bfloat16 or wider, within the bound.
No kernel may reach another device: no remote copies, remote signals or barrier semaphores. Data moves between devices by JAX's collectives and lax.ppermute only.
A program may use at most 64 MiB of HBM per device.

```python
import math
import jax
import jax.numpy as jnp
from jax import lax

DIM = 64
LEAF = 512
RANK = 256
RHS = 32
NEAR = 4
FAR = 4
ITERS = 2
LEAF_DEV = 16
NLEAF = 2048
NPTS = 1048576
NODES1 = 512
NODES2 = 128


def block_cliques(key, blocks):
    row_keys = jax.random.split(key, blocks)
    shuffled = jax.vmap(lambda single: jax.random.permutation(single, 16))(row_keys).astype(jnp.int32)
    position = jnp.argsort(shuffled, axis=1, stable=True).astype(jnp.int32)
    group_of = position // 4
    offset = position % 4
    turn_steps = jnp.arange(4, dtype=jnp.int32)
    slot_index = group_of[:, :, None] * 4 + (offset[:, :, None] + turn_steps[None, None, :]) % 4
    picked = jax.vmap(lambda values, places: values[places])(shuffled, slot_index)
    base_ids = (jnp.arange(blocks, dtype=jnp.int32) * 16)[:, None, None]
    return (picked + base_ids).reshape(blocks * 16, 4).astype(jnp.int32)


def distinct_rows(key, rows, choices, taken):
    row_keys = jax.random.split(key, rows)
    shuffled = jax.vmap(lambda single: jax.random.permutation(single, choices))(row_keys)
    return shuffled[:, :taken].astype(jnp.int32)


def draw_points(key, part):
    key = jax.random.fold_in(key, 17)
    values = jnp.clip(jax.random.normal(key, (DIM, NPTS), jnp.float32), -6.0, 6.0)
    return values.astype(jnp.bfloat16)


def draw_tree_order(key, part):
    key = jax.random.fold_in(key, 19)
    span = LEAF * LEAF_DEV
    blocks = NPTS // span
    shuffled = distinct_rows(key, blocks, span, span)
    return shuffled.reshape(NPTS).astype(jnp.int32)


def draw_leaf_skel(key, part):
    key = jax.random.fold_in(key, 23)
    return distinct_rows(key, NLEAF, LEAF, RANK)


def draw_skel_mid(key, part):
    key = jax.random.fold_in(key, 29)
    return distinct_rows(key, NODES1, 4 * RANK, RANK)


def draw_skel_top(key, part):
    key = jax.random.fold_in(key, 31)
    return distinct_rows(key, NODES2, 4 * RANK, RANK)


def draw_near_lists(key, part):
    key = jax.random.fold_in(key, 37)
    return block_cliques(key, NLEAF // 16)


def draw_far_mid(key, part):
    key = jax.random.fold_in(key, 41)
    return block_cliques(key, NODES1 // 16)


def draw_far_top(key, part):
    key = jax.random.fold_in(key, 43)
    return block_cliques(key, NODES2 // 16)


def block_levels(own_key, extent, shards, low, high):
    def one(axis_at, shards_of):
        draws = jax.random.uniform(jax.random.fold_in(jax.random.fold_in(own_key, 6), axis_at), (shards_of,), jnp.float32, low / len(shards), high / len(shards))
        return jnp.repeat(jnp.exp(draws), extent[axis_at] // shards_of).reshape((-1,) + (1,) * (len(extent) - axis_at - 1))

    loudness = one(*shards[0])
    for cut in shards[1:]:
        loudness = loudness * one(*cut)
    return loudness


def centred(key, dims, width, limit, pieces=(), kind=jnp.bfloat16):
    result = jax.random.normal(key, dims, jnp.float32) * width
    if len(pieces) > 0:
        result = block_levels(key, dims, pieces, -0.22, 0.18) * result
    return jnp.clip(result, min=-limit, max=limit).astype(kind)


def setup_inputs(seed: int = 0) -> dict:
    keys = jax.random.split(jax.random.key(seed), 13)
    return {
        "points": draw_points(jax.random.fold_in(keys[12], 71), 0),
        "tree_order": draw_tree_order(jax.random.fold_in(keys[12], 71), 0),
        "rhs": centred(keys[2], (RHS, NPTS), 1.0, 6.0, ((1, 128),), jnp.float32),
        "leaf_skel": draw_leaf_skel(jax.random.fold_in(keys[12], 71), 0),
        "skel_mid": draw_skel_mid(jax.random.fold_in(keys[12], 71), 0),
        "skel_top": draw_skel_top(jax.random.fold_in(keys[12], 71), 0),
        "near_lists": draw_near_lists(jax.random.fold_in(keys[12], 71), 0),
        "far_mid": draw_far_mid(jax.random.fold_in(keys[12], 71), 0),
        "far_top": draw_far_top(jax.random.fold_in(keys[12], 71), 0),
        "leaf_interp": centred(keys[9], (NLEAF, RANK, LEAF), LEAF ** -0.5, 0.25, ((0, 128),)),
        "interp_mid": centred(keys[10], (NODES1, RANK, 4 * RANK), (4 * RANK) ** -0.5, 0.1875, ((0, 128),)),
        "interp_top": centred(keys[11], (NODES1, RANK, RANK), (4 * RANK) ** -0.5, 0.1875, ((0, 128),)),
    }


ridge_shift = 1.0
highest = lax.Precision.HIGHEST

def kernel_tile(source, target):
    left_side = source.astype(jnp.float32)
    right_side = target.astype(jnp.float32)
    products = jnp.einsum('da,db->ab', left_side, right_side, precision=highest)
    squared = lax.optimization_barrier(jnp.sum(left_side * left_side, axis=0))[:, None] + lax.optimization_barrier(jnp.sum(right_side * right_side, axis=0))[None, :] - 2.0 * products
    return jnp.exp(-(2.0 / DIM) * squared).astype(jnp.bfloat16)

def interact(weights_all, coords_all, node_lists):

    def one_node(node_row):
        target = coords_all[node_row]
        running = jnp.zeros((weights_all.shape[1], coords_all.shape[2]), jnp.float32)
        for member in range(node_lists.shape[1]):
            source = node_lists[node_row, member]
            running = running + jnp.dot(weights_all[source].astype(jnp.float32), kernel_tile(coords_all[source], target).astype(jnp.float32), preferred_element_type=jnp.float32)
        return running
    return lax.map(one_node, jnp.arange(node_lists.shape[0], dtype=jnp.int32))

def join_children(values):
    parents = values.shape[0] // 4
    grouped = values.reshape(parents, 4, values.shape[1], values.shape[2])
    return jnp.transpose(grouped, (0, 2, 1, 3)).reshape(parents, values.shape[1], 4 * values.shape[2])

def gram_of(left_block, right_block):
    return jnp.einsum('ap,bp->ab', left_block, right_block, precision=highest)

def block_solve(gram_block, values):
    factor = jnp.linalg.cholesky(gram_block)
    return jax.scipy.linalg.cho_solve((factor, True), values)

def reference(points, tree_order, rhs, leaf_skel, skel_mid, skel_top, near_lists, far_mid, far_top, leaf_interp, interp_mid, interp_top):
    near_scale = 32.0 / math.sqrt(LEAF * NEAR)
    far_scale = 64.0 / math.sqrt(RANK * FAR)
    block_span = LEAF * LEAF_DEV
    positions = jnp.arange(NPTS, dtype=jnp.int32)
    source_index = (positions // block_span * block_span + tree_order).astype(jnp.int32)
    tree_points = points[:, source_index]
    tree_rhs = rhs[:, source_index]
    leaf_points = jnp.transpose(tree_points.reshape(DIM, NLEAF, LEAF), (1, 0, 2))
    coords_leaf = jnp.take_along_axis(leaf_points, leaf_skel[:, None, :], axis=2)
    coords_mid = jnp.take_along_axis(join_children(coords_leaf), skel_mid[:, None, :], axis=2)
    coords_top = jnp.take_along_axis(join_children(coords_mid), skel_top[:, None, :], axis=2)
    leaf_float = leaf_interp.astype(jnp.float32)
    mid_float = interp_mid.astype(jnp.float32)
    top_float = interp_top.astype(jnp.float32)

    def apply_operator(direction):
        weights = jnp.transpose(direction.astype(jnp.bfloat16).reshape(RHS, NLEAF, LEAF), (1, 0, 2))
        skel_leaf = jnp.einsum('krp,ksp->krs', weights.astype(jnp.float32), leaf_float, precision=highest).astype(jnp.bfloat16)
        skel_one = jnp.einsum('nrc,nsc->nrs', join_children(skel_leaf).astype(jnp.float32), mid_float, precision=highest).astype(jnp.bfloat16)
        top_terms = jnp.einsum('nrc,nsc->nrs', skel_one.astype(jnp.float32), top_float, precision=highest)
        skel_two = lax.optimization_barrier(jnp.sum(top_terms.reshape(NODES2, 4, RHS, RANK), axis=1)).astype(jnp.bfloat16)
        down_two = (far_scale * interact(skel_two, coords_top, far_top)).astype(jnp.bfloat16)
        parents = down_two[jnp.arange(NODES1) // 4].astype(jnp.float32)
        down_one = far_scale * interact(skel_one, coords_mid, far_mid) + jnp.einsum('nrs,nsc->nrc', parents, top_float, precision=highest)
        down_one = down_one.astype(jnp.bfloat16)
        down_leaf = jnp.einsum('nrs,nsc->nrc', down_one.astype(jnp.float32), mid_float, precision=highest).astype(jnp.bfloat16)
        down_leaf = jnp.transpose(down_leaf.reshape(NODES1, RHS, 4, RANK), (0, 2, 1, 3)).reshape(NLEAF, RHS, RANK)
        far_terms = jnp.einsum('ksr,krp->ksp', down_leaf.astype(jnp.float32), leaf_float, precision=highest)
        near_terms = interact(weights, leaf_points, near_lists)
        summed = near_scale * near_terms + far_terms
        return ridge_shift * direction + jnp.transpose(summed, (1, 0, 2)).reshape(RHS, NPTS)
    solution = jnp.zeros_like(tree_rhs)
    residual = tree_rhs
    direction = tree_rhs
    rho_now = gram_of(residual, residual)
    for iteration in range(ITERS):
        image = apply_operator(direction)
        gram_block = gram_of(direction, image)
        gram_block = 0.5 * (gram_block + gram_block.T)
        alpha_block = block_solve(gram_block, rho_now)
        solution = solution + jnp.einsum('ab,ap->bp', alpha_block, direction, precision=highest)
        residual = residual - jnp.einsum('ab,ap->bp', alpha_block, image, precision=highest)
        if iteration + 1 < ITERS:
            rho_next = gram_of(residual, residual)
            beta_block = block_solve(rho_now, rho_next)
            direction = residual + jnp.einsum('ab,ap->bp', beta_block, direction, precision=highest)
            rho_now = rho_next
    solution_out = jnp.zeros_like(tree_rhs).at[:, source_index].set(solution)
    residual_out = jnp.zeros_like(tree_rhs).at[:, source_index].set(residual)
    return (solution_out, residual_out)
```

```python
import math

import jax
import jax.numpy as jnp
from jax import lax
from jax.experimental import pallas as pl
from jax.experimental.pallas import tpu as pltpu
from jax.sharding import PartitionSpec as P

AXES = ("outer", "inner")
f32 = jnp.float32
bf16 = jnp.bfloat16
HIGHEST = lax.Precision.HIGHEST

DIM = 64
LEAVES = 16
LEAF = 512
SPAN = LEAVES * LEAF
RANK = 256
SIDES = 32
MID = 4
LIST = 4
LANES = 128
SQ = DIM
RHS_LANE = LANES - SIDES
EXPO = -(2.0 / DIM) * math.log2(math.e)
NEAR_SCALE = 32.0 / math.sqrt(LEAF * LIST)
FAR_SCALE = 64.0 / math.sqrt(RANK * LIST)

C1_ROWS = MID * RANK
S1_AT = C1_ROWS
S_HALF = SIDES
S1_ROWS = MID * 2 * S_HALF
MID_ROWS = C1_ROWS + S1_ROWS
S2_AT = MID_ROWS + RANK
S2_ROWS = 2 * S_HALF
PAY_ROWS = S2_AT + S2_ROWS
TOP_ROWS = RANK + S2_ROWS
PAY2_ROWS = S1_ROWS + S2_ROWS

VM = pl.BlockSpec(memory_space=pltpu.VMEM)
SM = pl.BlockSpec(memory_space=pltpu.SMEM)
ANY = pl.BlockSpec(memory_space=pl.ANY)


def params(mib):
    return pltpu.CompilerParams(vmem_limit_bytes=mib * 2**20)


def nt(left, right):
    return lax.dot_general(left, right, (((1,), (1,)), ((), ())), preferred_element_type=f32)


def nn(left, right):
    return jnp.dot(left, right, preferred_element_type=f32)


def target_side(rows):
    lane = lax.broadcasted_iota(jnp.int32, rows.shape, 1)
    values = rows.astype(f32)
    shifted = pltpu.roll(values, 3, 1)
    other = jnp.where(lane < SQ + 3, 1.0, jnp.where(lane < SQ + 6, shifted, 0.0))
    return jnp.where(lane < SQ, -2.0 * values, other).astype(bf16)


def tile(source_rows, target_rows):
    return jnp.exp2(EXPO * nt(source_rows, target_rows)).astype(bf16)


def split(values):
    high = values.astype(bf16)
    return high, (values - high.astype(f32)).astype(bf16)


def climb(s0_ref, mid_ref, top_ref, pay_ref, s1_at, s2_at):
    total = jnp.zeros((SIDES, RANK), f32)
    for node in range(MID):
        joined = jnp.concatenate([s0_ref[4 * node + k] for k in range(4)], axis=1)
        s1 = nt(joined, mid_ref[node]).astype(bf16)
        for half in range(2):
            at = s1_at + (2 * node + half) * S_HALF
            pay_ref[at : at + S_HALF, :] = s1[:, half * LANES : (half + 1) * LANES]
        total = total + nt(s1, top_ref[node])
    s2 = total.astype(bf16)
    for half in range(2):
        at = s2_at + half * S_HALF
        pay_ref[at : at + S_HALF, :] = s2[:, half * LANES : (half + 1) * LANES]


def setup_kernel(
    order, leaf_skel, skel_mid, skel_top, near, points, rhs, leaf_hbm, mid_hbm, top_hbm,
    a_out, b_out, r_out, pay, perm, inv,
    rows, tree, skel, leaf_v, mid_v, top_v, s0, sources, sems,
):
    copies = [
        pltpu.make_async_copy(leaf_hbm, leaf_v, sems.at[0]),
        pltpu.make_async_copy(mid_hbm, mid_v, sems.at[1]),
        pltpu.make_async_copy(top_hbm, top_v, sems.at[2]),
    ]
    for copy in copies:
        copy.start()

    count = jnp.int32(0)
    for leaf in range(LEAVES):
        members = [near[leaf, m] & (LEAVES - 1) for m in range(LIST)]
        first = jnp.minimum(jnp.minimum(members[0], members[1]), jnp.minimum(members[2], members[3]))
        leads = first == leaf

        @pl.when(leads)
        def _(members=members, count=count):
            for m in range(LIST):
                perm[count * LIST + m] = members[m]
                inv[members[m]] = count * LIST + m

        count = count + leads.astype(jnp.int32)

    def turn(step, _):
        at = pl.multiple_of(step * LEAF, LEAF)
        values = points[:, pl.ds(at, LEAF)].astype(f32)
        square = jnp.sum(values * values, axis=0, keepdims=True)
        high = square.astype(bf16).astype(f32)
        middle = (square - high).astype(bf16).astype(f32)
        low = square - high - middle
        row = lax.broadcasted_iota(jnp.int32, (SIDES, LEAF), 0)
        extra = jnp.where(row == 0, high, jnp.where(row == 1, middle, jnp.where(row == 2, low, jnp.where(row < 6, 1.0, 0.0))))
        stacked = jnp.concatenate([values, extra, rhs[:, pl.ds(at, LEAF)]], axis=0)
        rows[pl.ds(at, LEAF), :] = stacked.T
        return 0

    lax.fori_loop(0, LEAVES, turn, 0)

    unroll = 32

    def pick_mid(step, _):
        base = step * unroll
        node = base // RANK
        for u in range(unroll):
            at = node * 4 * RANK + skel_mid[base + u]
            source = order[(at // RANK) * LEAF + leaf_skel[at]]
            sources[base + u] = source
            skel[pl.ds(base + u, 1), :] = rows[pl.ds(source, 1), :]
        return 0

    lax.fori_loop(0, C1_ROWS // unroll, pick_mid, 0)

    def pick_top(step, _):
        base = step * unroll
        for u in range(unroll):
            source = sources[skel_top[base + u]]
            skel[pl.ds(C1_ROWS + base + u, 1), :] = rows[pl.ds(source, 1), :]
        return 0

    lax.fori_loop(0, RANK // unroll, pick_top, 0)
    pay[0:C1_ROWS, :] = skel[0:C1_ROWS, :].astype(bf16)
    pay[MID_ROWS:S2_AT, :] = skel[C1_ROWS:, :].astype(bf16)

    for copy in copies:
        copy.wait()

    def one_leaf(place, _):
        leaf = perm[place]
        base = leaf * LEAF

        def pick(step, _):
            at = step * 64
            for u in range(64):
                tree[pl.ds(at + u, 1), :] = rows[pl.ds(order[base + at + u], 1), :]
            return 0

        lax.fori_loop(0, LEAF // 64, pick, 0)
        values = tree[...]
        a_out[place] = values.astype(bf16)
        b_out[place] = target_side(values)
        right = values.T[RHS_LANE:, :]
        r_out[place] = right
        s0[leaf] = nt(right.astype(bf16), leaf_v[leaf]).astype(bf16)
        return 0

    lax.fori_loop(0, LEAVES, one_leaf, 0)
    climb(s0, mid_v, top_v, pay, S1_AT, S2_AT)


def setup(order, leaf_skel, skel_mid, skel_top, near, points, rhs, leaf_interp, interp_mid, interp_top):
    return pl.pallas_call(
        setup_kernel,
        out_shape=[
            jax.ShapeDtypeStruct((LEAVES, LEAF, LANES), bf16),
            jax.ShapeDtypeStruct((LEAVES, LEAF, LANES), bf16),
            jax.ShapeDtypeStruct((LEAVES, SIDES, LEAF), f32),
            jax.ShapeDtypeStruct((PAY_ROWS, LANES), bf16),
            jax.ShapeDtypeStruct((LEAVES,), jnp.int32),
            jax.ShapeDtypeStruct((LEAVES,), jnp.int32),
        ],
        in_specs=[SM] * 5 + [VM] * 2 + [ANY] * 3,
        out_specs=[VM] * 4 + [SM] * 2,
        scratch_shapes=[
            pltpu.VMEM((SPAN, LANES), f32),
            pltpu.VMEM((LEAF, LANES), f32),
            pltpu.VMEM((C1_ROWS + RANK, LANES), f32),
            pltpu.VMEM((LEAVES, RANK, LEAF), bf16),
            pltpu.VMEM((MID, RANK, 4 * RANK), bf16),
            pltpu.VMEM((MID, RANK, RANK), bf16),
            pltpu.VMEM((LEAVES, SIDES, RANK), bf16),
            pltpu.SMEM((C1_ROWS,), jnp.int32),
            pltpu.SemaphoreType.DMA((3,)),
        ],
        compiler_params=params(40),
    )(order, leaf_skel, skel_mid, skel_top, near, points, rhs, leaf_interp, interp_mid, interp_top)


def near_first_kernel(a_ref, b_ref, r_ref, out, tiles):
    member = pl.program_id(0) % LIST

    @pl.when(member == 0)
    def _():
        out[...] = jnp.zeros_like(out)

    sources = a_ref[0]
    weights = r_ref[0].astype(bf16)
    for target in range(LIST):
        block = tile(sources, b_ref[target])
        tiles[0, :, target * LEAF : (target + 1) * LEAF] = block
        out[target] += nn(weights, block)


def near_first(a_rows, b_rows, right):
    return pl.pallas_call(
        near_first_kernel,
        grid=(LEAVES,),
        out_shape=[
            jax.ShapeDtypeStruct((LEAVES, SIDES, LEAF), f32),
            jax.ShapeDtypeStruct((LEAVES, LEAF, LIST * LEAF), bf16),
        ],
        in_specs=[
            pl.BlockSpec((1, LEAF, LANES), lambda i: (i, 0, 0)),
            pl.BlockSpec((LIST, LEAF, LANES), lambda i: (i // LIST, 0, 0)),
            pl.BlockSpec((1, SIDES, LEAF), lambda i: (i, 0, 0)),
        ],
        out_specs=[
            pl.BlockSpec((LIST, SIDES, LEAF), lambda i: (i // LIST, 0, 0)),
            pl.BlockSpec((1, LEAF, LIST * LEAF), lambda i: (i, 0, 0)),
        ],
        compiler_params=params(40),
    )(a_rows, b_rows, right)


def near_second_kernel(tiles, q_ref, out):
    member = pl.program_id(0) % LIST

    @pl.when(member == 0)
    def _():
        out[...] = jnp.zeros_like(out)

    both = jnp.concatenate(split(q_ref[0]), axis=0)
    for target in range(LIST):
        product = nn(both, tiles[0, :, target * LEAF : (target + 1) * LEAF])
        out[target] += product[:SIDES] + product[SIDES:]


def near_second(tiles, image):
    return pl.pallas_call(
        near_second_kernel,
        grid=(LEAVES,),
        out_shape=jax.ShapeDtypeStruct((LEAVES, SIDES, LEAF), f32),
        in_specs=[
            pl.BlockSpec((1, LEAF, LIST * LEAF), lambda i: (i, 0, 0)),
            pl.BlockSpec((1, SIDES, LEAF), lambda i: (i, 0, 0)),
        ],
        out_specs=pl.BlockSpec((LIST, SIDES, LEAF), lambda i: (i // LIST, 0, 0)),
        compiler_params=params(40),
    )(tiles, image)


def descend(mid_far, top_far, inv, mid_v, top_v, leaf_v, base_ref, near_ref, out):
    u2 = (FAR_SCALE * top_far).astype(bf16)
    for node in range(MID):
        u1 = (FAR_SCALE * mid_far[node] + nn(u2, top_v[node])).astype(bf16)
        u0 = nn(u1, mid_v[node]).astype(bf16)
        for k in range(4):
            leaf = 4 * node + k
            place = inv[leaf]
            far = nn(u0[:, k * RANK : (k + 1) * RANK], leaf_v[leaf])
            out[place] = base_ref[place] + NEAR_SCALE * near_ref[place] + far


def far_first_kernel(
    ids, far_mid, far_top, inv, pair_a, pair_b, eight_a, eight_b, leaf_hbm, mid_hbm, top_hbm, right, near,
    q_out, pay, mid_tiles, top_tiles,
    four, sixteen, leaf_v, mid_v, top_v, s0, sems,
):
    pool_copies = [
        pltpu.make_async_copy(pair_a, four.at[0:2], sems.at[0]),
        pltpu.make_async_copy(pair_b, four.at[2:4], sems.at[1]),
        pltpu.make_async_copy(eight_a, sixteen.at[0:8], sems.at[2]),
        pltpu.make_async_copy(eight_b, sixteen.at[8:16], sems.at[3]),
    ]
    own_copies = [
        pltpu.make_async_copy(leaf_hbm, leaf_v, sems.at[4]),
        pltpu.make_async_copy(mid_hbm, mid_v, sems.at[5]),
        pltpu.make_async_copy(top_hbm, top_v, sems.at[6]),
    ]
    for copy in pool_copies + own_copies:
        copy.start()
    for copy in pool_copies:
        copy.wait()
    device = ids[0]

    top_far = jnp.zeros((SIDES, RANK), f32)
    target = target_side(sixteen[0, 0:RANK, :])
    for m in range(LIST):
        slot = (far_top[m] ^ device) & 15
        slot = slot ^ (((slot >> 2) & 1) << 1)
        block = tile(sixteen[slot, 0:RANK, :], target)
        top_tiles[m] = block
        for half in range(2):
            weights = sixteen[slot, RANK + half * S_HALF : RANK + (half + 1) * S_HALF, :]
            top_far = top_far + nn(weights, block[half * LANES : (half + 1) * LANES, :])
    mid_far = []
    for node in range(MID):
        total = jnp.zeros((SIDES, RANK), f32)
        target = target_side(four[0, node * RANK : (node + 1) * RANK, :])
        for m in range(LIST):
            entry = far_mid[node, m] & 15
            slot = (entry >> 2) ^ (device & 3)
            local = entry & 3
            block = tile(four[slot, pl.ds(pl.multiple_of(local * RANK, RANK), RANK), :], target)
            mid_tiles[node * LIST + m] = block
            for half in range(2):
                at = pl.multiple_of(S1_AT + (2 * local + half) * S_HALF, S_HALF)
                weights = four[slot, pl.ds(at, S_HALF), :]
                total = total + nn(weights, block[half * LANES : (half + 1) * LANES, :])
        mid_far.append(total)
    for copy in own_copies:
        copy.wait()
    descend(mid_far, top_far, inv, mid_v, top_v, leaf_v, right, near, q_out)
    for leaf in range(LEAVES):
        both = jnp.concatenate(split(q_out[inv[leaf]]), axis=0)
        raised = nt(both, leaf_v[leaf])
        s0[leaf] = (raised[:SIDES] + raised[SIDES:]).astype(bf16)
    climb(s0, mid_v, top_v, pay, 0, S1_ROWS)


def interp_scratch():
    return [
        pltpu.VMEM((LEAVES, RANK, LEAF), bf16),
        pltpu.VMEM((MID, RANK, 4 * RANK), bf16),
        pltpu.VMEM((MID, RANK, RANK), bf16),
    ]


def far_first(ids, far_mid, far_top, inv, pair_a, pair_b, eight_a, eight_b, leaf_interp, interp_mid, interp_top, right, near):
    return pl.pallas_call(
        far_first_kernel,
        out_shape=[
            jax.ShapeDtypeStruct((LEAVES, SIDES, LEAF), f32),
            jax.ShapeDtypeStruct((PAY2_ROWS, LANES), bf16),
            jax.ShapeDtypeStruct((MID * LIST, RANK, RANK), bf16),
            jax.ShapeDtypeStruct((LIST, RANK, RANK), bf16),
        ],
        in_specs=[SM] * 4 + [ANY] * 7 + [VM] * 2,
        out_specs=[VM] * 4,
        scratch_shapes=[
            pltpu.VMEM((4, PAY_ROWS, LANES), bf16),
            pltpu.VMEM((16, TOP_ROWS, LANES), bf16),
            *interp_scratch(),
            pltpu.VMEM((LEAVES, SIDES, RANK), bf16),
            pltpu.SemaphoreType.DMA((7,)),
        ],
        compiler_params=params(40),
    )(ids, far_mid, far_top, inv, pair_a, pair_b, eight_a, eight_b, leaf_interp, interp_mid, interp_top, right, near)


def far_second_kernel(
    ids, far_mid, far_top, inv, pair_a, pair_b, eight_a, eight_b, mid_tiles, top_tiles, leaf_hbm, mid_hbm, top_hbm,
    right, image, near,
    p_out, gram,
    four, sixteen, leaf_v, mid_v, top_v, sems,
):
    own_copies = [
        pltpu.make_async_copy(leaf_hbm, leaf_v, sems.at[4]),
        pltpu.make_async_copy(mid_hbm, mid_v, sems.at[5]),
        pltpu.make_async_copy(top_hbm, top_v, sems.at[6]),
    ]
    for copy in own_copies:
        copy.start()
    four[0:2] = pair_a[...]
    four[2:4] = pair_b[...]
    sixteen[0:8] = eight_a[...]
    sixteen[8:16] = eight_b[...]
    device = ids[0]
    top_far = jnp.zeros((SIDES, RANK), f32)
    for m in range(LIST):
        slot = (far_top[m] ^ device) & 15
        slot = slot ^ (((slot >> 2) & 1) << 1)
        for half in range(2):
            weights = sixteen[slot, half * S_HALF : (half + 1) * S_HALF, :]
            top_far = top_far + nn(weights, top_tiles[m, half * LANES : (half + 1) * LANES, :])
    mid_far = []
    for node in range(MID):
        total = jnp.zeros((SIDES, RANK), f32)
        for m in range(LIST):
            entry = far_mid[node, m] & 15
            slot = (entry >> 2) ^ (device & 3)
            local = entry & 3
            for half in range(2):
                at = pl.multiple_of((2 * local + half) * S_HALF, S_HALF)
                weights = four[slot, pl.ds(at, S_HALF), :]
                total = total + nn(weights, mid_tiles[node * LIST + m, half * LANES : (half + 1) * LANES, :])
        mid_far.append(total)
    for copy in own_copies:
        copy.wait()
    descend(mid_far, top_far, inv, mid_v, top_v, leaf_v, image, near, p_out)
    total = jnp.zeros((2 * SIDES, 3 * SIDES), f32)
    for place in range(LEAVES):
        left = jnp.concatenate([right[place], image[place]], axis=0)
        all_three = jnp.concatenate([left, p_out[place]], axis=0)
        total = total + lax.dot_general(
            left, all_three, (((1,), (1,)), ((), ())), preferred_element_type=f32, precision=HIGHEST
        )
    gram[...] = total


def far_second(ids, far_mid, far_top, inv, pools, mid_tiles, top_tiles, leaf_interp, interp_mid, interp_top, right, image, near):
    return pl.pallas_call(
        far_second_kernel,
        out_shape=[
            jax.ShapeDtypeStruct((LEAVES, SIDES, LEAF), f32),
            jax.ShapeDtypeStruct((2 * SIDES, 3 * SIDES), f32),
        ],
        in_specs=[SM] * 4 + [VM] * 6 + [ANY] * 3 + [VM] * 3,
        out_specs=[VM] * 2,
        scratch_shapes=[
            pltpu.VMEM((4, PAY2_ROWS, LANES), bf16),
            pltpu.VMEM((16, S2_ROWS, LANES), bf16),
            *interp_scratch(),
            pltpu.SemaphoreType.DMA((7,)),
        ],
        compiler_params=params(40),
    )(ids, far_mid, far_top, inv, *pools, mid_tiles, top_tiles, leaf_interp, interp_mid, interp_top, right, image, near)


def unsort_kernel(order, perm, image, second, out, tree, rows):
    def one_leaf(place, _):
        base = perm[place] * LEAF
        stacked = jnp.concatenate([image[place], second[place], jnp.zeros((2 * SIDES, LEAF), f32)], axis=0)
        tree[...] = stacked.T

        def put(step, _):
            at = step * 64
            for u in range(64):
                rows[pl.ds(order[base + at + u], 1), :] = tree[pl.ds(at + u, 1), :]
            return 0

        lax.fori_loop(0, LEAF // 64, put, 0)
        return 0

    lax.fori_loop(0, LEAVES, one_leaf, 0)

    def turn(step, _):
        at = pl.multiple_of(step * LEAF, LEAF)
        out[:, pl.ds(at, LEAF)] = rows[pl.ds(at, LEAF), :].T[: 2 * SIDES, :]
        return 0

    lax.fori_loop(0, LEAVES, turn, 0)


def unsort(order, perm, image, second):
    return pl.pallas_call(
        unsort_kernel,
        out_shape=jax.ShapeDtypeStruct((2 * SIDES, SPAN), f32),
        in_specs=[SM] * 2 + [VM] * 2,
        out_specs=VM,
        scratch_shapes=[pltpu.VMEM((LEAF, LANES), f32), pltpu.VMEM((SPAN, LANES), f32)],
        compiler_params=params(40),
    )(order, perm, image, second)


def dot(left, right, contract=(1, 0)):
    return lax.dot_general(
        left, right, (((contract[0],), (contract[1],)), ((), ())), preferred_element_type=f32, precision=HIGHEST
    )


def eliminate(systems):
    row = lax.broadcasted_iota(jnp.int32, (SIDES, 1), 0)
    for k in range(SIDES):
        following = []
        for matrix, values in systems:
            scale = 1.0 / matrix[k : k + 1, k : k + 1]
            column = matrix[:, k : k + 1]
            matrix_row = matrix[k : k + 1, :] * scale
            values_row = values[k : k + 1, :] * scale
            following.append((
                jnp.where(row == k, matrix_row, matrix - column * matrix_row),
                jnp.where(row == k, values_row, values - column * values_row),
            ))
        systems = following
    return [values for _, values in systems]


def finish_kernel(gram, mapped, rhs, x_out, r_out):
    n = SIDES
    rr, rq, rp = gram[0:n, 0:n], gram[0:n, n : 2 * n], gram[0:n, 2 * n : 3 * n]
    qr, qq, qp = gram[n : 2 * n, 0:n], gram[n : 2 * n, n : 2 * n], gram[n : 2 * n, 2 * n : 3 * n]
    eye = (lax.broadcasted_iota(jnp.int32, (n, n), 0) == lax.broadcasted_iota(jnp.int32, (n, n), 1)).astype(f32)
    alpha, rr_inverse = eliminate([(0.5 * (rq + qr), rr), (rr, eye)])
    rq_alpha = dot(rq, alpha)
    rho = rr - rq_alpha - dot(alpha, qr, (0, 0)) + dot(alpha, dot(qq, alpha), (0, 0))
    first = eye + dot(rr_inverse, rho)
    half = dot(first, dot(rq, first) - dot(rp, alpha), (0, 0)) - dot(alpha, dot(qq, first) - dot(qp, alpha), (0, 0))
    turned = dot(half, eye, (0, 0))
    (beta,) = eliminate([(0.5 * (half + turned), rho)])
    c0 = alpha + dot(first, beta)
    c1 = -dot(alpha, beta)

    lane = lax.broadcasted_iota(jnp.int32, (n, LANES), 1)
    place = lax.broadcasted_iota(jnp.int32, (n, LANES), 0)
    to_x = ((lane & 63) == place).astype(f32)
    to_r = ((lane & 63) == place + n).astype(f32)
    combine = jnp.concatenate(
        [dot(c0, to_x), dot(c1, to_x) - dot(c0, to_r), -dot(c1, to_r), jnp.zeros((n, LANES), f32)], axis=0
    ).T
    high, low = split(combine)
    upper = lax.broadcasted_iota(jnp.int32, (LANES, LANES), 0) < 2 * n
    both = jnp.where(upper, high.astype(f32), low.astype(f32)).astype(bf16)
    both = jnp.concatenate([both, both], axis=1)

    def column(step, _):
        at = pl.multiple_of(step * LEAF, LEAF)
        right = rhs[:, pl.ds(at, LEAF)]
        stacked = jnp.concatenate([right, mapped[:, pl.ds(at, LEAF)], jnp.zeros((n, LEAF), f32)], axis=0)
        result = nn(both, jnp.concatenate(split(stacked), axis=0))
        result = result[: 2 * n] + result[2 * n :]
        x_out[:, pl.ds(at, LEAF)] = result[:n]
        r_out[:, pl.ds(at, LEAF)] = right + result[n:]
        return 0

    lax.fori_loop(0, LEAVES, column, 0)


def finish(gram, mapped, rhs):
    return pl.pallas_call(
        finish_kernel,
        out_shape=[jax.ShapeDtypeStruct((SIDES, SPAN), f32)] * 2,
        in_specs=[VM] * 3,
        out_specs=[VM] * 2,
        compiler_params=params(40),
    )(gram, mapped, rhs)


def swapped(value, mask):
    count = lax.axis_size(AXES)
    return lax.ppermute(value, AXES, [(source, source ^ mask) for source in range(count)])


def gather_pools(payload, top_at):
    pair = jnp.stack([payload, swapped(payload, 1)])
    other_pair = swapped(pair, 2)
    four = jnp.concatenate([pair[:, top_at:], other_pair[:, top_at:]])
    eight = jnp.concatenate([four, swapped(four, 6)])
    return pair, other_pair, eight, swapped(eight, 8)


def shards(
    points, tree_order, rhs, leaf_skel, skel_mid, skel_top, near_lists, far_mid, far_top,
    leaf_interp, interp_mid, interp_top,
):
    device = lax.axis_index(AXES)
    top_row = lax.dynamic_index_in_dim(skel_top, device, 0, keepdims=False)
    far_row = lax.dynamic_index_in_dim(far_top, device, 0, keepdims=False)
    ids = device.astype(jnp.int32).reshape(1)
    interps = (leaf_interp, interp_mid, interp_top)
    a_rows, b_rows, right, payload, perm, inv = setup(
        tree_order, leaf_skel.reshape(-1), skel_mid.reshape(-1), top_row, near_lists, points, rhs, *interps
    )
    pools = gather_pools(payload, MID_ROWS)
    near, tiles = near_first(a_rows, b_rows, right)
    image, payload, mid_tiles, top_tiles = far_first(ids, far_mid, far_row, inv, *pools, *interps, right, near)
    pools = gather_pools(payload, S1_ROWS)
    near = near_second(tiles, image)
    second, gram = far_second(ids, far_mid, far_row, inv, pools, mid_tiles, top_tiles, *interps, right, image, near)
    mapped = unsort(tree_order, perm, image, second)
    for mask in (1, 2, 6, 8, 24, 32, 96):
        gram = gram + swapped(gram, mask)
    return tuple(finish(gram, mapped, rhs))


def solution(mesh):
    placed = (
        P(None, AXES), P(AXES), P(None, AXES), P(AXES, None), P(AXES, None), P(), P(AXES, None), P(AXES, None), P(),
        P(AXES, None, None), P(AXES, None, None), P(AXES, None, None),
    )
    return jax.shard_map(
        shards, mesh=mesh, in_specs=placed, out_specs=(P(None, AXES), P(None, AXES)), check_vma=False
    )
```

```python
import math

import jax
import jax.numpy as jnp
from jax import lax
from jax.experimental import pallas as pl
from jax.experimental.pallas import tpu as pltpu
from jax.sharding import PartitionSpec as P

AXES = ("outer", "inner")
f32 = jnp.float32
bf16 = jnp.bfloat16
HIGHEST = lax.Precision.HIGHEST

DIM = 64
LEAVES = 16
LEAF = 512
SPAN = LEAVES * LEAF
RANK = 256
SIDES = 32
MID = 4
LIST = 4
LANES = 128
SQ = DIM
RHS_LANE = LANES - SIDES
EXPO = -(2.0 / DIM) * math.log2(math.e)
NEAR_SCALE = 32.0 / math.sqrt(LEAF * LIST)
FAR_SCALE = 64.0 / math.sqrt(RANK * LIST)

C_ROWS = RANK // 2 + 2 * 16
S_ROWS = 2 * SIDES
S1_AT = MID * C_ROWS
MID_ROWS = MID * (C_ROWS + S_ROWS)
S2_AT = MID_ROWS + C_ROWS
PAY_ROWS = S2_AT + S_ROWS
TOP_ROWS = C_ROWS + S_ROWS
S1_ROWS = MID * S_ROWS
PAY2_ROWS = S1_ROWS + S_ROWS
GROUPS = LEAVES // LIST
PAIRS = [(p, q) for p in range(LIST) for q in range(p, LIST)]

VM = pl.BlockSpec(memory_space=pltpu.VMEM)
SM = pl.BlockSpec(memory_space=pltpu.SMEM)
HBM = pl.BlockSpec(memory_space=pltpu.HBM)


def params(mib):
    return pltpu.CompilerParams(vmem_limit_bytes=mib * 2**20)


def in_hbm(*arrays):
    return [pltpu.with_memory_space_constraint(array, pltpu.HBM) for array in arrays]


def lasting(microseconds):
    return pl.CostEstimate(flops=int(1.15e9 * microseconds), bytes_accessed=0, transcendentals=0)


def nt(left, right):
    return lax.dot_general(left, right, (((1,), (1,)), ((), ())), preferred_element_type=f32)


def nn(left, right):
    return jnp.dot(left, right, preferred_element_type=f32)


def target_side(rows):
    lane = lax.broadcasted_iota(jnp.int32, rows.shape, 1)
    values = rows.astype(f32)
    shifted = pltpu.roll(values, 3, 1)
    other = jnp.where(lane < SQ + 3, 1.0, jnp.where(lane < SQ + 6, shifted, 0.0))
    return jnp.where(lane < SQ, -2.0 * values, other).astype(bf16)


def tile(source_rows, target_rows):
    return jnp.exp2(EXPO * nt(source_rows, target_rows)).astype(bf16)


def split(values):
    high = values.astype(bf16)
    return high, (values - high.astype(f32)).astype(bf16)


def halves(pay_ref, at, values):
    for half in range(2):
        pay_ref[at + half * SIDES : at + (half + 1) * SIDES, :] = values[:, half * LANES : (half + 1) * LANES]


def joined(ref, slot, at):
    return jnp.concatenate([ref[slot, pl.ds(at + half * SIDES, SIDES), :] for half in range(2)], axis=1)


def climb(s0_ref, mid_ref, top_ref, pay_ref, s1_at, s2_at):
    total = jnp.zeros((SIDES, RANK), f32)
    for node in range(MID):
        children = jnp.concatenate([s0_ref[4 * node + k] for k in range(4)], axis=1)
        s1 = nt(children, mid_ref[node]).astype(bf16)
        halves(pay_ref, s1_at + node * S_ROWS, s1)
        total = total + nt(s1, top_ref[node])
    halves(pay_ref, s2_at, total.astype(bf16))


def pack_points(pay_ref, at, rows):
    lane = lax.broadcasted_iota(jnp.int32, (LANES, LANES), 1)
    second = pltpu.roll(rows[LANES:, :], DIM, 1)
    pay_ref[at : at + LANES, :] = jnp.where(lane < DIM, rows[:LANES, :], second).astype(bf16)
    squares = rows.T[SQ : SQ + 16, :].astype(bf16)
    for half in range(2):
        start = at + LANES + 16 * half
        pay_ref[start : start + 16, :] = squares[:, half * LANES : (half + 1) * LANES]


def unpack_points(ref, slot, at):
    lane = lax.broadcasted_iota(jnp.int32, (LANES, LANES), 1)
    packed = ref[slot, pl.ds(at, LANES), :].astype(f32)
    points = jnp.concatenate([packed, pltpu.roll(packed, DIM, 1)], axis=0)
    lane = lax.broadcasted_iota(jnp.int32, (RANK, LANES), 1)
    points = jnp.where(lane < DIM, points, jnp.where(lane < DIM + 3, 1.0, 0.0)).astype(bf16)
    squares = jnp.concatenate([ref[slot, pl.ds(at + LANES + 16 * half, 16), :] for half in range(2)], axis=1).astype(f32)
    return points, squares[0:1] + squares[1:2] + squares[2:3]


def far_tile(target, source):
    points, squares = source
    return jnp.exp2(EXPO * (nt(target, points) + squares)).astype(bf16)


def far_target(points, squares):
    lane = lax.broadcasted_iota(jnp.int32, (RANK, LANES), 1)
    values = points.astype(f32)
    columns = jnp.concatenate([squares, jnp.zeros((7, RANK), f32)], axis=0).T
    column = columns[:, 0:1]
    high = column.astype(bf16).astype(f32)
    middle = (column - high).astype(bf16).astype(f32)
    low = column - high - middle
    parts = jnp.where(lane == SQ, high, jnp.where(lane == SQ + 1, middle, jnp.where(lane == SQ + 2, low, 0.0)))
    return jnp.where(lane < SQ, -2.0 * values, parts).astype(bf16)


def setup_kernel(
    leaf_skel, skel_mid, near, order_hbm, skel_top_hbm, points_hbm, rhs_hbm, leaf_hbm, mid_hbm, top_hbm,
    a_out, b_out, r_out, pay, perm,
    order, skel_top, points, rhs, rows, tree, skel, leaf_v, mid_v, top_v, s0, sources, sems,
):
    device = this_device()
    eight = pl.multiple_of(device // 8 * 8, 8)
    quarter = SPAN // 4
    small = [
        pltpu.make_async_copy(order_hbm, order, sems.at[0]),
        pltpu.make_async_copy(skel_top_hbm.at[pl.ds(eight, 8), :], skel_top, sems.at[1]),
    ]
    chunks = []
    for i in range(4):
        part = pl.ds(i * quarter, quarter)
        chunks.append([
            pltpu.make_async_copy(points_hbm.at[:, part], points.at[:, part], sems.at[2 + i]),
            pltpu.make_async_copy(rhs_hbm.at[:, part], rhs.at[:, part], sems.at[6 + i]),
        ])
    large = [
        pltpu.make_async_copy(leaf_hbm, leaf_v, sems.at[10]),
        pltpu.make_async_copy(mid_hbm, mid_v, sems.at[11]),
        pltpu.make_async_copy(top_hbm, top_v, sems.at[12]),
    ]
    for copy in small + sum(chunks, []) + large:
        copy.start()

    count = jnp.int32(0)
    for leaf in range(LEAVES):
        members = [near[m, leaf] & (LEAVES - 1) for m in range(LIST)]
        first = jnp.minimum(jnp.minimum(members[0], members[1]), jnp.minimum(members[2], members[3]))
        leads = first == leaf

        @pl.when(leads)
        def _(members=members, count=count):
            for m in range(LIST):
                perm[count * LIST + m] = members[m]

        count = count + leads.astype(jnp.int32)

    def turn(step, _):
        at = pl.multiple_of(step * LEAF, LEAF)
        values = points[:, pl.ds(at, LEAF)].astype(f32)
        square = jnp.sum(values * values, axis=0, keepdims=True)
        high = square.astype(bf16).astype(f32)
        middle = (square - high).astype(bf16).astype(f32)
        low = square - high - middle
        row = lax.broadcasted_iota(jnp.int32, (SIDES, LEAF), 0)
        extra = jnp.where(row == 0, high, jnp.where(row == 1, middle, jnp.where(row == 2, low, jnp.where(row < 6, 1.0, 0.0))))
        stacked = jnp.concatenate([values, extra, rhs[:, pl.ds(at, LEAF)]], axis=0)
        rows[pl.ds(at, LEAF), :] = stacked.T
        return 0

    for i in range(4):
        for copy in chunks[i]:
            copy.wait()
        lax.fori_loop(4 * i, 4 * i + 4, turn, 0)
    for copy in small:
        copy.wait()

    unroll = 16

    for node in range(MID):
        def pick_mid(step, _, node=node):
            base = step * unroll
            spots = [skel_mid[node, base + u] for u in range(unroll)]
            leaves = [4 * node + (at >> 8) for at in spots]
            inner = [leaf_skel[leaf, at & (RANK - 1)] for leaf, at in zip(leaves, spots)]
            found = [order[leaf * LEAF + at] for leaf, at in zip(leaves, inner)]
            for u in range(unroll):
                skel[pl.ds(node * RANK + base + u, 1), :] = rows[pl.ds(found[u], 1), :]
            for u in range(unroll):
                sources[node * RANK + base + u] = found[u]
            return 0

        lax.fori_loop(0, RANK // unroll, pick_mid, 0)

    own = device & 7

    def pick_top(step, _):
        base = step * unroll
        spots = [skel_top[own, base + u] for u in range(unroll)]
        found = [sources[at] for at in spots]
        for u in range(unroll):
            skel[pl.ds(MID * RANK + base + u, 1), :] = rows[pl.ds(found[u], 1), :]
        return 0

    lax.fori_loop(0, RANK // unroll, pick_top, 0)
    for node in range(MID + 1):
        pack_points(pay, MID_ROWS if node == MID else node * C_ROWS, skel[node * RANK : (node + 1) * RANK, :])

    for copy in large:
        copy.wait()

    def one_leaf(place, _):
        leaf = perm[place]
        base = leaf * LEAF

        def pick(step, _):
            at = step * 64
            for u in range(64):
                source = order[base + at + u]
                tree[pl.ds(at + u, 1), :] = rows[pl.ds(source, 1), :]
            return 0

        lax.fori_loop(0, LEAF // 64, pick, 0)
        values = tree[...]
        a_out[place] = values.astype(bf16)
        b_out[place] = target_side(values)
        right = values.T[RHS_LANE:, :]
        r_out[place] = right
        s0[leaf] = nt(right.astype(bf16), leaf_v[leaf]).astype(bf16)
        return 0

    lax.fori_loop(0, LEAVES, one_leaf, 0)
    climb(s0, mid_v, top_v, pay, S1_AT, S2_AT)


def interp_scratch():
    return [
        pltpu.VMEM((LEAVES, RANK, LEAF), bf16),
        pltpu.VMEM((MID, RANK, 4 * RANK), bf16),
        pltpu.VMEM((MID, RANK, RANK), bf16),
    ]


def setup(leaf_skel, skel_mid, near, order, skel_top, points, rhs, interps):
    order, skel_top, points, rhs, *interps = in_hbm(order, skel_top, points, rhs, *interps)
    return pl.pallas_call(
        setup_kernel,
        out_shape=[
            jax.ShapeDtypeStruct((LEAVES, LEAF, LANES), bf16),
            jax.ShapeDtypeStruct((LEAVES, LEAF, LANES), bf16),
            jax.ShapeDtypeStruct((LEAVES, SIDES, LEAF), f32),
            jax.ShapeDtypeStruct((PAY_ROWS, LANES), bf16),
            jax.ShapeDtypeStruct((LEAVES,), jnp.int32),
        ],
        in_specs=[SM] * 3 + [HBM] * 7,
        out_specs=[VM] * 4 + [SM],
        scratch_shapes=[
            pltpu.SMEM((SPAN,), jnp.int32),
            pltpu.SMEM((8, RANK), jnp.int32),
            pltpu.VMEM((DIM, SPAN), bf16),
            pltpu.VMEM((SIDES, SPAN), f32),
            pltpu.VMEM((SPAN, LANES), f32),
            pltpu.VMEM((LEAF, LANES), f32),
            pltpu.VMEM(((MID + 1) * RANK, LANES), f32),
            *interp_scratch(),
            pltpu.VMEM((LEAVES, SIDES, RANK), bf16),
            pltpu.SMEM((MID * RANK,), jnp.int32),
            pltpu.SemaphoreType.DMA((13,)),
        ],
        compiler_params=params(32),
        cost_estimate=lasting(20),
    )(leaf_skel, skel_mid, near, order, skel_top, points, rhs, *interps)


def apply_near(weights, tiles, out):
    for target in range(LIST):
        total = jnp.zeros((weights[0].shape[0], LEAF), f32)
        for source in range(LIST):
            block = tiles[PAIRS.index((min(source, target), max(source, target)))]
            total = total + (nn if source <= target else nt)(weights[source], block)
        out[target] = total if total.shape[0] == SIDES else total[:SIDES] + total[SIDES:]


def near_first(group, a_rows, b_rows, right):
    def kernel(a_ref, b_ref, r_ref, out, tiles):
        for i, (p, q) in enumerate(PAIRS):
            tiles[i] = tile(a_ref[LIST * group + p], b_ref[LIST * group + q])
        apply_near([r_ref[LIST * group + s].astype(bf16) for s in range(LIST)], tiles, out)

    return pl.pallas_call(
        kernel,
        out_shape=[
            jax.ShapeDtypeStruct((LIST, SIDES, LEAF), f32),
            jax.ShapeDtypeStruct((len(PAIRS), LEAF, LEAF), bf16),
        ],
        in_specs=[VM] * 3,
        out_specs=[VM] * 2,
        compiler_params=params(16),
        cost_estimate=lasting(3.3),
    )(a_rows, b_rows, right)


def near_second(group, tiles, image):
    def kernel(tiles_ref, q_ref, out):
        weights = [jnp.concatenate(split(q_ref[LIST * group + s]), axis=0) for s in range(LIST)]
        apply_near(weights, tiles_ref, out)

    return pl.pallas_call(
        kernel,
        out_shape=jax.ShapeDtypeStruct((LIST, SIDES, LEAF), f32),
        in_specs=[VM] * 2,
        out_specs=VM,
        compiler_params=params(16),
        cost_estimate=lasting(2.6),
    )(tiles, image)


def descend(mid_far, top_far, perm, mid_v, top_v, leaf_v, u0, base_ref, near_refs, out):
    u2 = (FAR_SCALE * top_far).astype(bf16)
    for node in range(MID):
        u1 = (FAR_SCALE * mid_far[node] + nn(u2, top_v[node])).astype(bf16)
        down = nn(u1, mid_v[node]).astype(bf16)
        for k in range(4):
            u0[4 * node + k] = down[:, k * RANK : (k + 1) * RANK]
    for place in range(LEAVES):
        leaf = perm[place]
        far = nn(u0[leaf], leaf_v[leaf])
        out[place] = base_ref[place] + NEAR_SCALE * near_refs[place // LIST][place % LIST] + far


def top_slot(entry, device):
    mask = (entry ^ device) & 15
    ring = ((mask >> 1) & 1) ^ ((mask >> 2) & 1)
    return ring | (((mask >> 2) & 1) << 1) | (((mask >> 3) & 1) << 2) | ((mask & 1) << 3)


def mid_slot(entry, device):
    mask = ((entry >> 2) ^ device) & 3
    return (mask >> 1) | ((mask & 1) << 1)


def this_device():
    return lax.axis_index("outer") * lax.axis_size("inner") + lax.axis_index("inner")


def pool_copies(pair_a, pair_b, eight_a, eight_b, four, sixteen, sems):
    return [
        pltpu.make_async_copy(pair_a, four.at[0:2], sems.at[0]),
        pltpu.make_async_copy(pair_b, four.at[2:4], sems.at[1]),
        pltpu.make_async_copy(eight_a, sixteen.at[0:8], sems.at[2]),
        pltpu.make_async_copy(eight_b, sixteen.at[8:16], sems.at[3]),
    ]


def far_first_kernel(
    far_mid, far_top, perm, pair_a, pair_b, eight_a, eight_b, leaf_v, mid_v, top_v, right, near0, near1, near2, near3,
    q_out, pay, mid_tiles, top_tiles,
    four, sixteen, s0, sems,
):
    pools = pool_copies(pair_a, pair_b, eight_a, eight_b, four, sixteen, sems)
    for copy in pools:
        copy.start()
    for copy in pools:
        copy.wait()
    device = this_device()

    target = far_target(*unpack_points(sixteen, 0, 0))
    top_far = jnp.zeros((SIDES, RANK), f32)
    for m in range(LIST):
        slot = top_slot(far_top[m, device], device)
        block = far_tile(target, unpack_points(sixteen, slot, 0))
        top_tiles[m] = block
        top_far = top_far + nt(joined(sixteen, slot, C_ROWS), block)
    mid_far = []
    for node in range(MID):
        target = far_target(*unpack_points(four, 0, node * C_ROWS))
        total = jnp.zeros((SIDES, RANK), f32)
        for m in range(LIST):
            entry = far_mid[node, m]
            slot = mid_slot(entry, device)
            local = entry & 3
            block = far_tile(target, unpack_points(four, slot, pl.multiple_of(local * C_ROWS, C_ROWS)))
            mid_tiles[node * LIST + m] = block
            total = total + nt(joined(four, slot, pl.multiple_of(S1_AT + local * S_ROWS, S_ROWS)), block)
        mid_far.append(total)
    descend(mid_far, top_far, perm, mid_v, top_v, leaf_v, s0, right, (near0, near1, near2, near3), q_out)
    for place in range(LEAVES):
        leaf = perm[place]
        raised = nt(jnp.concatenate(split(q_out[place]), axis=0), leaf_v[leaf])
        s0[leaf] = (raised[:SIDES] + raised[SIDES:]).astype(bf16)
    climb(s0, mid_v, top_v, pay, 0, S1_ROWS)


def far_first(far_mid, far_top, perm, pools, interps, right, near):
    return pl.pallas_call(
        far_first_kernel,
        out_shape=[
            jax.ShapeDtypeStruct((LEAVES, SIDES, LEAF), f32),
            jax.ShapeDtypeStruct((PAY2_ROWS, LANES), bf16),
            jax.ShapeDtypeStruct((MID * LIST, RANK, RANK), bf16),
            jax.ShapeDtypeStruct((LIST, RANK, RANK), bf16),
        ],
        in_specs=[SM] * 3 + [pl.BlockSpec(memory_space=pl.ANY)] * 4 + [VM] * 8,
        out_specs=[VM] * 4,
        scratch_shapes=[
            pltpu.VMEM((4, PAY_ROWS, LANES), bf16),
            pltpu.VMEM((16, TOP_ROWS, LANES), bf16),
            pltpu.VMEM((LEAVES, SIDES, RANK), bf16),
            pltpu.SemaphoreType.DMA((4,)),
        ],
        compiler_params=params(14),
        cost_estimate=lasting(8),
    )(far_mid, far_top, perm, *pools, *interps, right, *near)


def far_second_kernel(
    far_mid, far_top, perm, pair_a, pair_b, eight_a, eight_b, leaf_v, mid_v, top_v, mid_tiles, top_tiles,
    right, image, near0, near1, near2, near3,
    p_out, gram,
    four, sixteen, u0, sems,
):
    pools = pool_copies(pair_a, pair_b, eight_a, eight_b, four, sixteen, sems)
    for copy in pools:
        copy.start()
    for copy in pools:
        copy.wait()
    device = this_device()
    top_far = jnp.zeros((SIDES, RANK), f32)
    for m in range(LIST):
        top_far = top_far + nt(joined(sixteen, top_slot(far_top[m, device], device), 0), top_tiles[m])
    mid_far = []
    for node in range(MID):
        total = jnp.zeros((SIDES, RANK), f32)
        for m in range(LIST):
            entry = far_mid[node, m]
            weights = joined(four, mid_slot(entry, device), pl.multiple_of((entry & 3) * S_ROWS, S_ROWS))
            total = total + nt(weights, mid_tiles[node * LIST + m])
        mid_far.append(total)
    descend(mid_far, top_far, perm, mid_v, top_v, leaf_v, u0, image, (near0, near1, near2, near3), p_out)
    total = jnp.zeros((4 * SIDES, 6 * SIDES), f32)
    for place in range(LEAVES):
        parts = [split(ref[place]) for ref in (right, image, p_out)]
        left = jnp.concatenate([part[i] for i in range(2) for part in parts[:2]], axis=0)
        total = total + nt(left, jnp.concatenate([part[i] for i in range(2) for part in parts], axis=0))
    total = total[: 2 * SIDES] + total[2 * SIDES :]
    turned = total.T
    total = (turned[: 3 * SIDES] + turned[3 * SIDES :]).T
    gram[...] = total


def far_second(far_mid, far_top, perm, pools, interps, mid_tiles, top_tiles, right, image, near):
    return pl.pallas_call(
        far_second_kernel,
        out_shape=[
            jax.ShapeDtypeStruct((LEAVES, SIDES, LEAF), f32),
            jax.ShapeDtypeStruct((2 * SIDES, 3 * SIDES), f32),
        ],
        in_specs=[SM] * 3 + [pl.BlockSpec(memory_space=pl.ANY)] * 4 + [VM] * 11,
        out_specs=[VM] * 2,
        scratch_shapes=[
            pltpu.VMEM((4, PAY2_ROWS, LANES), bf16),
            pltpu.VMEM((16, S_ROWS, LANES), bf16),
            pltpu.VMEM((LEAVES, SIDES, RANK), bf16),
            pltpu.SemaphoreType.DMA((4,)),
        ],
        compiler_params=params(14),
        cost_estimate=lasting(8),
    )(far_mid, far_top, perm, *pools, *interps, mid_tiles, top_tiles, right, image, *near)


PARTS = 2
PART = SPAN // PARTS


def put_back(group, order, perm, image, second, rows):
    def kernel(order_ref, perm_ref, q_ref, p_ref, *refs):
        out, tree = refs[-2:]
        for member in range(LIST):
            place = LIST * group + member
            stacked = jnp.concatenate([q_ref[place], p_ref[place], jnp.zeros((2 * SIDES, LEAF), f32)], axis=0)
            tree[member * LEAF : (member + 1) * LEAF, :] = stacked.T

        for member in range(LIST):
            base = perm_ref[LIST * group + member] * LEAF

            def put(step, _, member=member, base=base):
                at = step * 64
                for u in range(64):
                    out[pl.ds(order_ref[base + at + u], 1), :] = tree[pl.ds(member * LEAF + at + u, 1), :]
                return 0

            lax.fori_loop(0, LEAF // 64, put, 0)

    earlier = [] if rows is None else [rows]
    return pl.pallas_call(
        kernel, out_shape=jax.ShapeDtypeStruct((SPAN, LANES), f32),
        in_specs=[SM] * 2 + [VM] * (2 + len(earlier)), out_specs=VM,
        scratch_shapes=[pltpu.VMEM((LIST * LEAF, LANES), f32)],
        input_output_aliases={4: 0} if earlier else {},
        compiler_params=params(12), cost_estimate=lasting(2.5),
    )(order, perm, image, second, *earlier)


def to_columns(part, rows):
    def kernel(rows_ref, out):
        for i in range(PART // LEAF):
            at = part * PART + i * LEAF
            out[:, i * LEAF : (i + 1) * LEAF] = rows_ref[at : at + LEAF, :].T[: 2 * SIDES, :]

    return pl.pallas_call(
        kernel, out_shape=jax.ShapeDtypeStruct((2 * SIDES, PART), f32), in_specs=[VM], out_specs=VM,
        compiler_params=params(12), cost_estimate=lasting(2),
    )(rows)


def dot(left, right, contract=(1, 0)):
    return lax.dot_general(
        left, right, (((contract[0],), (contract[1],)), ((), ())), preferred_element_type=f32, precision=HIGHEST
    )


def eliminate(systems):
    row = lax.broadcasted_iota(jnp.int32, (SIDES, 1), 0)
    for k in range(SIDES):
        following = []
        for matrix, values in systems:
            scale = 1.0 / matrix[k : k + 1, k : k + 1]
            column = matrix[:, k : k + 1]
            matrix_row = matrix[k : k + 1, :] * scale
            values_row = values[k : k + 1, :] * scale
            following.append((
                jnp.where(row == k, matrix_row, matrix - column * matrix_row),
                jnp.where(row == k, values_row, values - column * values_row),
            ))
        systems = following
    return [values for _, values in systems]


def finish_kernel(gram, rhs, mapped0, mapped1, x_out, r_out):
    n = SIDES
    rr, rq, rp = gram[0:n, 0:n], gram[0:n, n : 2 * n], gram[0:n, 2 * n : 3 * n]
    qr, qq, qp = gram[n : 2 * n, 0:n], gram[n : 2 * n, n : 2 * n], gram[n : 2 * n, 2 * n : 3 * n]
    eye = (lax.broadcasted_iota(jnp.int32, (n, n), 0) == lax.broadcasted_iota(jnp.int32, (n, n), 1)).astype(f32)
    alpha, rr_inverse = eliminate([(0.5 * (rq + qr), rr), (rr, eye)])
    rq_alpha = dot(rq, alpha)
    rho = rr - rq_alpha - dot(alpha, qr, (0, 0)) + dot(alpha, dot(qq, alpha), (0, 0))
    first = eye + dot(rr_inverse, rho)
    half = dot(first, dot(rq, first) - dot(rp, alpha), (0, 0)) - dot(alpha, dot(qq, first) - dot(qp, alpha), (0, 0))
    turned = dot(half, eye, (0, 0))
    (beta,) = eliminate([(0.5 * (half + turned), rho)])
    c0 = alpha + dot(first, beta)
    c1 = -dot(alpha, beta)

    lane = lax.broadcasted_iota(jnp.int32, (n, LANES), 1)
    place = lax.broadcasted_iota(jnp.int32, (n, LANES), 0)
    to_x = ((lane & 63) == place).astype(f32)
    to_r = ((lane & 63) == place + n).astype(f32)
    combine = jnp.concatenate(
        [dot(c0, to_x), dot(c1, to_x) - dot(c0, to_r), -dot(c1, to_r), jnp.zeros((n, LANES), f32)], axis=0
    ).T
    high, low = split(combine)
    upper = lax.broadcasted_iota(jnp.int32, (LANES, LANES), 0) < 2 * n
    both = jnp.where(upper, high.astype(f32), low.astype(f32)).astype(bf16)
    both = jnp.concatenate([both, both], axis=1)

    for i in range(LEAVES):
        span = slice(i * LEAF, (i + 1) * LEAF)
        part = (mapped0, mapped1)[i * LEAF // PART]
        at = i * LEAF % PART
        right = rhs[:, span]
        stacked = jnp.concatenate([right, part[:, at : at + LEAF], jnp.zeros((n, LEAF), f32)], axis=0)
        result = nn(both, jnp.concatenate(split(stacked), axis=0))
        result = result[: 2 * n] + result[2 * n :]
        x_out[:, span] = result[:n]
        r_out[:, span] = right + result[n:]


def finish(gram, rhs, mapped):
    return pl.pallas_call(
        finish_kernel,
        out_shape=[jax.ShapeDtypeStruct((SIDES, SPAN), f32)] * 2,
        in_specs=[VM] * 4,
        out_specs=[VM] * 2,
        compiler_params=params(24),
    )(gram, rhs, *mapped)


def swapped(value, mask):
    count = lax.axis_size(AXES)
    return lax.ppermute(value, AXES, [(source, source ^ mask) for source in range(count)])


def gather_pools(payload, top_at, inputs, steps):
    done = []

    def beside(step, values):
        nonlocal inputs
        arrived, results, inputs = lax.optimization_barrier((values, steps[step](inputs), inputs))
        done.append(results)
        return arrived

    pair = jnp.stack([payload, beside(0, swapped(payload, 2))])
    two = pair[:, top_at:]
    four = jnp.concatenate([two, beside(1, swapped(two, 6))])
    eight = jnp.concatenate([four, beside(2, swapped(four, 8))])
    other_pair, other_eight = beside(3, (swapped(pair, 1), swapped(eight, 1)))
    return (pair, other_pair, eight, other_eight), [result for results in done for result in results]


def shards(
    points, tree_order, rhs, leaf_skel, skel_mid, skel_top, near_lists, far_mid, far_top,
    leaf_interp, interp_mid, interp_top,
):
    interps = (leaf_interp, interp_mid, interp_top)
    a_rows, b_rows, right, payload, perm = setup(
        leaf_skel, skel_mid, near_lists.T, tree_order, skel_top, points, rhs, interps
    )
    def first(*groups):
        return lambda inputs: [near_first(group, *inputs) for group in groups]

    pools, found = gather_pools(payload, MID_ROWS, (a_rows, b_rows, right), [first(0, 1), first(2), first(3), first()])
    near, tiles = zip(*found)
    lists = (far_mid, far_top.T)
    image, payload, mid_tiles, top_tiles = far_first(*lists, perm, pools, interps, right, near)
    def again(*groups):
        return lambda inputs: [near_second(group, tiles[group], *inputs) for group in groups]

    pools, near = gather_pools(payload, S1_ROWS, (image,), [again(0), again(1), again(2), again(3)])
    second, gram = far_second(*lists, perm, pools, interps, mid_tiles, top_tiles, right, image, near)
    rows = None
    for group in range(GROUPS):
        rows = put_back(group, tree_order, perm, image, second, rows)
    mapped = [to_columns(part, rows) for part in range(PARTS)]
    for mask in (1, 2, 6, 8, 24, 32, 96):
        gram = gram + swapped(gram, mask)
    return tuple(finish(gram, rhs, mapped))


def solution(mesh):
    placed = (
        P(None, AXES), P(AXES), P(None, AXES), P(AXES, None), P(AXES, None), P(), P(AXES, None), P(AXES, None), P(),
        P(AXES, None, None), P(AXES, None, None), P(AXES, None, None),
    )
    return jax.shard_map(
        shards, mesh=mesh, in_specs=placed, out_specs=(P(None, AXES), P(None, AXES)), check_vma=False
    )
```

```python
import math

import jax
import jax.numpy as jnp
from jax import lax
from jax.experimental import pallas as pl
from jax.experimental.pallas import tpu as pltpu
from jax.sharding import PartitionSpec as P

AXES = ("outer", "inner")
f32 = jnp.float32
bf16 = jnp.bfloat16
HIGHEST = lax.Precision.HIGHEST

DIM = 64
LEAVES = 16
LEAF = 512
SPAN = LEAVES * LEAF
RANK = 256
SIDES = 32
MID = 4
LIST = 4
LANES = 128
SQ = DIM
RHS_LANE = LANES - SIDES
EXPO = -(2.0 / DIM) * math.log2(math.e)
NEAR_SCALE = 32.0 / math.sqrt(LEAF * LIST)
FAR_SCALE = 64.0 / math.sqrt(RANK * LIST)

C_ROWS = RANK // 2 + 2 * 16
S_ROWS = 2 * SIDES
S1_AT = MID * C_ROWS
MID_ROWS = MID * (C_ROWS + S_ROWS)
S2_AT = MID_ROWS + C_ROWS
PAY_ROWS = S2_AT + S_ROWS
TOP_ROWS = C_ROWS + S_ROWS
S1_ROWS = MID * S_ROWS
PAY2_ROWS = S1_ROWS + S_ROWS
GROUPS = LEAVES // LIST
SKEL_MID_AT = LEAVES * RANK
PAIRS = [(p, q) for p in range(LIST) for q in range(p, LIST)]

VM = pl.BlockSpec(memory_space=pltpu.VMEM)
SM = pl.BlockSpec(memory_space=pltpu.SMEM)
HBM = pl.BlockSpec(memory_space=pltpu.HBM)


def params(mib):
    return pltpu.CompilerParams(vmem_limit_bytes=mib * 2**20)


def in_hbm(*arrays):
    return [pltpu.with_memory_space_constraint(array, pltpu.HBM) for array in arrays]


def lasting(microseconds):
    return pl.CostEstimate(flops=int(1.15e9 * microseconds), bytes_accessed=0, transcendentals=0)


def nt(left, right):
    return lax.dot_general(left, right, (((1,), (1,)), ((), ())), preferred_element_type=f32)


def nn(left, right):
    return jnp.dot(left, right, preferred_element_type=f32)


def target_side(rows):
    lane = lax.broadcasted_iota(jnp.int32, rows.shape, 1)
    values = rows.astype(f32)
    shifted = pltpu.roll(values, 3, 1)
    other = jnp.where(lane < SQ + 3, 1.0, jnp.where(lane < SQ + 6, shifted, 0.0))
    return jnp.where(lane < SQ, -2.0 * values, other).astype(bf16)


def tile(source_rows, target_rows):
    return jnp.exp2(EXPO * nt(source_rows, target_rows)).astype(bf16)


def split(values):
    high = values.astype(bf16)
    return high, (values - high.astype(f32)).astype(bf16)


def halves(pay_ref, at, values):
    for half in range(2):
        pay_ref[at + half * SIDES : at + (half + 1) * SIDES, :] = values[:, half * LANES : (half + 1) * LANES]


def joined(ref, slot, at):
    return jnp.concatenate([ref[slot, pl.ds(at + half * SIDES, SIDES), :] for half in range(2)], axis=1)


def climb(s0_ref, mid_ref, top_ref, pay_ref, s1_at, s2_at):
    total = jnp.zeros((SIDES, RANK), f32)
    for node in range(MID):
        children = jnp.concatenate([s0_ref[4 * node + k] for k in range(4)], axis=1)
        s1 = nt(children, mid_ref[node]).astype(bf16)
        halves(pay_ref, s1_at + node * S_ROWS, s1)
        total = total + nt(s1, top_ref[node])
    halves(pay_ref, s2_at, total.astype(bf16))


def pack_points(pay_ref, at, rows):
    lane = lax.broadcasted_iota(jnp.int32, (LANES, LANES), 1)
    second = pltpu.roll(rows[LANES:, :], DIM, 1)
    pay_ref[at : at + LANES, :] = jnp.where(lane < DIM, rows[:LANES, :], second).astype(bf16)
    squares = rows.T[SQ : SQ + 16, :].astype(bf16)
    for half in range(2):
        start = at + LANES + 16 * half
        pay_ref[start : start + 16, :] = squares[:, half * LANES : (half + 1) * LANES]


def unpack_points(ref, slot, at):
    lane = lax.broadcasted_iota(jnp.int32, (LANES, LANES), 1)
    packed = ref[slot, pl.ds(at, LANES), :].astype(f32)
    points = jnp.concatenate([packed, pltpu.roll(packed, DIM, 1)], axis=0)
    lane = lax.broadcasted_iota(jnp.int32, (RANK, LANES), 1)
    points = jnp.where(lane < DIM, points, jnp.where(lane < DIM + 3, 1.0, 0.0)).astype(bf16)
    squares = jnp.concatenate([ref[slot, pl.ds(at + LANES + 16 * half, 16), :] for half in range(2)], axis=1).astype(f32)
    return points, squares[0:1] + squares[1:2] + squares[2:3]


def far_tile(target, source):
    points, squares = source
    return jnp.exp2(EXPO * (nt(target, points) + squares)).astype(bf16)


def far_target(points, squares):
    lane = lax.broadcasted_iota(jnp.int32, (RANK, LANES), 1)
    values = points.astype(f32)
    columns = jnp.concatenate([squares, jnp.zeros((7, RANK), f32)], axis=0).T
    column = columns[:, 0:1]
    high = column.astype(bf16).astype(f32)
    middle = (column - high).astype(bf16).astype(f32)
    low = column - high - middle
    parts = jnp.where(lane == SQ, high, jnp.where(lane == SQ + 1, middle, jnp.where(lane == SQ + 2, low, 0.0)))
    return jnp.where(lane < SQ, -2.0 * values, parts).astype(bf16)


def setup_kernel(
    leaf_skel_hbm, skel_mid_hbm, near_hbm, order_hbm, skel_top_hbm, points_hbm, rhs_hbm, leaf_hbm, mid_hbm, top_hbm,
    a_out, b_out, r_out, pay, perm,
    lists, near, order, skel_top, points, rhs, rows, tree, skel, leaf_v, mid_v, top_v, s0, sources, sems,
):
    device = this_device()
    eight = pl.multiple_of(device // 8 * 8, 8)
    quarter = SPAN // 4
    small = [
        pltpu.make_async_copy(order_hbm, order, sems.at[0]),
        pltpu.make_async_copy(skel_top_hbm.at[pl.ds(eight, 8), :], skel_top, sems.at[1]),
    ]
    chunks = []
    for i in range(4):
        part = pl.ds(i * quarter, quarter)
        chunks.append([
            pltpu.make_async_copy(points_hbm.at[:, part], points.at[:, part], sems.at[2 + i]),
            pltpu.make_async_copy(rhs_hbm.at[:, part], rhs.at[:, part], sems.at[6 + i]),
        ])
    large = [
        pltpu.make_async_copy(leaf_hbm, leaf_v, sems.at[10]),
        pltpu.make_async_copy(mid_hbm, mid_v, sems.at[11]),
        pltpu.make_async_copy(top_hbm, top_v, sems.at[12]),
    ]
    small.append(pltpu.make_async_copy(near_hbm, near, sems.at[13]))
    for i in range(LEAVES):
        small.append(pltpu.make_async_copy(leaf_skel_hbm.at[i], lists.at[pl.ds(i * RANK, RANK)], sems.at[14 + i]))
    for i in range(MID):
        part = lists.at[pl.ds(SKEL_MID_AT + i * RANK, RANK)]
        small.append(pltpu.make_async_copy(skel_mid_hbm.at[i], part, sems.at[14 + LEAVES + i]))
    for copy in sum(chunks, []) + small:
        copy.start()

    def turn(step, _):
        at = pl.multiple_of(step * LEAF, LEAF)
        values = points[:, pl.ds(at, LEAF)].astype(f32)
        square = jnp.sum(values * values, axis=0, keepdims=True)
        high = square.astype(bf16).astype(f32)
        middle = (square - high).astype(bf16).astype(f32)
        low = square - high - middle
        row = lax.broadcasted_iota(jnp.int32, (SIDES, LEAF), 0)
        extra = jnp.where(row == 0, high, jnp.where(row == 1, middle, jnp.where(row == 2, low, jnp.where(row < 6, 1.0, 0.0))))
        stacked = jnp.concatenate([values, extra, rhs[:, pl.ds(at, LEAF)]], axis=0)
        rows[pl.ds(at, LEAF), :] = stacked.T
        return 0

    for i in range(4):
        for copy in chunks[i]:
            copy.wait()
        lax.fori_loop(4 * i, 4 * i + 4, turn, 0)
    for copy in large:
        copy.start()
    for copy in small:
        copy.wait()

    count = jnp.int32(0)
    for leaf in range(LEAVES):
        members = [near[m, leaf] & (LEAVES - 1) for m in range(LIST)]
        first = jnp.minimum(jnp.minimum(members[0], members[1]), jnp.minimum(members[2], members[3]))
        leads = first == leaf

        @pl.when(leads)
        def _(members=members, count=count):
            for m in range(LIST):
                perm[count * LIST + m] = members[m]

        count = count + leads.astype(jnp.int32)

    unroll = 32

    def pick_mid(step, _):
        base = step * unroll
        first = (base >> 8) * (4 * RANK)
        spots = [first + lists[SKEL_MID_AT + base + u] for u in range(unroll)]
        found = [order[((at >> 8) << 9) + lists[at]] for at in spots]
        for u in range(unroll):
            skel[pl.ds(base + u, 1), :] = rows[pl.ds(found[u], 1), :]
        for u in range(unroll):
            sources[base + u] = found[u]
        return 0

    lax.fori_loop(0, MID * RANK // unroll, pick_mid, 0)

    own = device & 7

    def pick_top(step, _):
        base = step * unroll
        spots = [skel_top[own, base + u] for u in range(unroll)]
        found = [sources[at] for at in spots]
        for u in range(unroll):
            skel[pl.ds(MID * RANK + base + u, 1), :] = rows[pl.ds(found[u], 1), :]
        return 0

    lax.fori_loop(0, RANK // unroll, pick_top, 0)
    for node in range(MID + 1):
        pack_points(pay, MID_ROWS if node == MID else node * C_ROWS, skel[node * RANK : (node + 1) * RANK, :])


    for copy in large:
        copy.wait()

    def one_leaf(place, _):
        leaf = perm[place]
        base = leaf * LEAF

        def pick(step, _):
            at = step * 64
            for u in range(64):
                tree[pl.ds(at + u, 1), :] = rows[pl.ds(order[base + at + u], 1), :]
            return 0

        lax.fori_loop(0, LEAF // 64, pick, 0)
        values = tree[...]
        a_out[place] = values.astype(bf16)
        b_out[place] = target_side(values)
        right = values.T[RHS_LANE:, :]
        r_out[place] = right
        s0[leaf] = nt(right.astype(bf16), leaf_v[leaf]).astype(bf16)
        return 0

    lax.fori_loop(0, LEAVES, one_leaf, 0)
    climb(s0, mid_v, top_v, pay, S1_AT, S2_AT)


def interp_scratch():
    return [
        pltpu.VMEM((LEAVES, RANK, LEAF), bf16),
        pltpu.VMEM((MID, RANK, 4 * RANK), bf16),
        pltpu.VMEM((MID, RANK, RANK), bf16),
    ]


def setup(leaf_skel, skel_mid, near, order, skel_top, points, rhs, interps):
    leaf_skel, skel_mid, near, order, skel_top, points, rhs, *interps = in_hbm(
        leaf_skel, skel_mid, near, order, skel_top, points, rhs, *interps
    )
    return pl.pallas_call(
        setup_kernel,
        out_shape=[
            jax.ShapeDtypeStruct((LEAVES, LEAF, LANES), bf16),
            jax.ShapeDtypeStruct((LEAVES, LEAF, LANES), bf16),
            jax.ShapeDtypeStruct((LEAVES, SIDES, LEAF), f32),
            jax.ShapeDtypeStruct((PAY_ROWS, LANES), bf16),
            jax.ShapeDtypeStruct((LEAVES,), jnp.int32),
        ],
        in_specs=[HBM] * 10,
        out_specs=[VM] * 4 + [SM],
        scratch_shapes=[
            pltpu.SMEM(((LEAVES + MID) * RANK,), jnp.int32),
            pltpu.SMEM((LIST, LEAVES), jnp.int32),
            pltpu.SMEM((SPAN,), jnp.int32),
            pltpu.SMEM((8, RANK), jnp.int32),
            pltpu.VMEM((DIM, SPAN), bf16),
            pltpu.VMEM((SIDES, SPAN), f32),
            pltpu.VMEM((SPAN, LANES), f32),
            pltpu.VMEM((LEAF, LANES), f32),
            pltpu.VMEM(((MID + 1) * RANK, LANES), f32),
            *interp_scratch(),
            pltpu.VMEM((LEAVES, SIDES, RANK), bf16),
            pltpu.SMEM((MID * RANK,), jnp.int32),
            pltpu.SemaphoreType.DMA((14 + LEAVES + MID,)),
        ],
        compiler_params=params(32),
        cost_estimate=lasting(20),
    )(leaf_skel, skel_mid, near, order, skel_top, points, rhs, *interps)


def apply_near(weights, tiles, out):
    for target in range(LIST):
        total = jnp.zeros((weights[0].shape[0], LEAF), f32)
        for source in range(LIST):
            block = tiles[PAIRS.index((min(source, target), max(source, target)))]
            total = total + (nn if source <= target else nt)(weights[source], block)
        out[target] = total if total.shape[0] == SIDES else total[:SIDES] + total[SIDES:]


def near_first(group, a_rows, b_rows, right):
    def kernel(a_ref, b_ref, r_ref, out, tiles):
        for i, (p, q) in enumerate(PAIRS):
            tiles[i] = tile(a_ref[LIST * group + p], b_ref[LIST * group + q])
        apply_near([r_ref[LIST * group + s].astype(bf16) for s in range(LIST)], tiles, out)

    return pl.pallas_call(
        kernel,
        out_shape=[
            jax.ShapeDtypeStruct((LIST, SIDES, LEAF), f32),
            jax.ShapeDtypeStruct((len(PAIRS), LEAF, LEAF), bf16),
        ],
        in_specs=[VM] * 3,
        out_specs=[VM] * 2,
        compiler_params=params(16),
        cost_estimate=lasting(3.3),
    )(a_rows, b_rows, right)


def near_second(group, tiles, image):
    def kernel(tiles_ref, q_ref, out):
        weights = [jnp.concatenate(split(q_ref[LIST * group + s]), axis=0) for s in range(LIST)]
        apply_near(weights, tiles_ref, out)

    return pl.pallas_call(
        kernel,
        out_shape=jax.ShapeDtypeStruct((LIST, SIDES, LEAF), f32),
        in_specs=[VM] * 2,
        out_specs=VM,
        compiler_params=params(16),
        cost_estimate=lasting(2.6),
    )(tiles, image)


def descend(mid_far, top_far, perm, mid_v, top_v, leaf_v, u0, base_ref, near_refs, out):
    u2 = (FAR_SCALE * top_far).astype(bf16)
    for node in range(MID):
        u1 = (FAR_SCALE * mid_far[node] + nn(u2, top_v[node])).astype(bf16)
        down = nn(u1, mid_v[node]).astype(bf16)
        for k in range(4):
            u0[4 * node + k] = down[:, k * RANK : (k + 1) * RANK]
    for place in range(LEAVES):
        leaf = perm[place]
        far = nn(u0[leaf], leaf_v[leaf])
        out[place] = base_ref[place] + NEAR_SCALE * near_refs[place // LIST][place % LIST] + far


def top_slot(entry, device):
    mask = (entry ^ device) & 15
    ring = ((mask >> 1) & 1) ^ ((mask >> 2) & 1)
    return ring | (((mask >> 2) & 1) << 1) | (((mask >> 3) & 1) << 2) | ((mask & 1) << 3)


def mid_slot(entry, device):
    mask = ((entry >> 2) ^ device) & 3
    return (mask >> 1) | ((mask & 1) << 1)


def this_device():
    return lax.axis_index("outer") * lax.axis_size("inner") + lax.axis_index("inner")


def pool_copies(pair_a, pair_b, eight_a, eight_b, four, sixteen, sems):
    return [
        pltpu.make_async_copy(pair_a, four.at[0:2], sems.at[0]),
        pltpu.make_async_copy(pair_b, four.at[2:4], sems.at[1]),
        pltpu.make_async_copy(eight_a, sixteen.at[0:8], sems.at[2]),
        pltpu.make_async_copy(eight_b, sixteen.at[8:16], sems.at[3]),
    ]


def far_first_kernel(
    far_mid, far_top, perm, pair_a, pair_b, eight_a, eight_b, leaf_v, mid_v, top_v, right, near0, near1, near2, near3,
    q_out, pay, mid_tiles, top_tiles,
    four, sixteen, s0, sems,
):
    pools = pool_copies(pair_a, pair_b, eight_a, eight_b, four, sixteen, sems)
    for copy in pools:
        copy.start()
    for copy in pools:
        copy.wait()
    device = this_device()

    target = far_target(*unpack_points(sixteen, 0, 0))
    top_far = jnp.zeros((SIDES, RANK), f32)
    for m in range(LIST):
        slot = top_slot(far_top[m, device], device)
        block = far_tile(target, unpack_points(sixteen, slot, 0))
        top_tiles[m] = block
        top_far = top_far + nt(joined(sixteen, slot, C_ROWS), block)
    mid_far = []
    for node in range(MID):
        target = far_target(*unpack_points(four, 0, node * C_ROWS))
        total = jnp.zeros((SIDES, RANK), f32)
        for m in range(LIST):
            entry = far_mid[node, m]
            slot = mid_slot(entry, device)
            local = entry & 3
            block = far_tile(target, unpack_points(four, slot, pl.multiple_of(local * C_ROWS, C_ROWS)))
            mid_tiles[node * LIST + m] = block
            total = total + nt(joined(four, slot, pl.multiple_of(S1_AT + local * S_ROWS, S_ROWS)), block)
        mid_far.append(total)
    descend(mid_far, top_far, perm, mid_v, top_v, leaf_v, s0, right, (near0, near1, near2, near3), q_out)
    for place in range(LEAVES):
        leaf = perm[place]
        raised = nt(jnp.concatenate(split(q_out[place]), axis=0), leaf_v[leaf])
        s0[leaf] = (raised[:SIDES] + raised[SIDES:]).astype(bf16)
    climb(s0, mid_v, top_v, pay, 0, S1_ROWS)


def far_first(far_mid, far_top, perm, pools, interps, right, near):
    return pl.pallas_call(
        far_first_kernel,
        out_shape=[
            jax.ShapeDtypeStruct((LEAVES, SIDES, LEAF), f32),
            jax.ShapeDtypeStruct((PAY2_ROWS, LANES), bf16),
            jax.ShapeDtypeStruct((MID * LIST, RANK, RANK), bf16),
            jax.ShapeDtypeStruct((LIST, RANK, RANK), bf16),
        ],
        in_specs=[SM] * 3 + [pl.BlockSpec(memory_space=pl.ANY)] * 4 + [VM] * 8,
        out_specs=[VM] * 4,
        scratch_shapes=[
            pltpu.VMEM((4, PAY_ROWS, LANES), bf16),
            pltpu.VMEM((16, TOP_ROWS, LANES), bf16),
            pltpu.VMEM((LEAVES, SIDES, RANK), bf16),
            pltpu.SemaphoreType.DMA((4,)),
        ],
        compiler_params=params(14),
        cost_estimate=lasting(8),
    )(far_mid, far_top, perm, *pools, *interps, right, *near)


def far_second_kernel(
    far_mid, far_top, perm, pair_a, pair_b, eight_a, eight_b, leaf_v, mid_v, top_v, mid_tiles, top_tiles,
    right, image, near0, near1, near2, near3,
    p_out, gram,
    four, sixteen, u0, sems,
):
    pools = pool_copies(pair_a, pair_b, eight_a, eight_b, four, sixteen, sems)
    for copy in pools:
        copy.start()
    for copy in pools:
        copy.wait()
    device = this_device()
    top_far = jnp.zeros((SIDES, RANK), f32)
    for m in range(LIST):
        top_far = top_far + nt(joined(sixteen, top_slot(far_top[m, device], device), 0), top_tiles[m])
    mid_far = []
    for node in range(MID):
        total = jnp.zeros((SIDES, RANK), f32)
        for m in range(LIST):
            entry = far_mid[node, m]
            weights = joined(four, mid_slot(entry, device), pl.multiple_of((entry & 3) * S_ROWS, S_ROWS))
            total = total + nt(weights, mid_tiles[node * LIST + m])
        mid_far.append(total)
    descend(mid_far, top_far, perm, mid_v, top_v, leaf_v, u0, image, (near0, near1, near2, near3), p_out)
    total = jnp.zeros((4 * SIDES, 6 * SIDES), f32)
    for place in range(LEAVES):
        parts = [split(ref[place]) for ref in (right, image, p_out)]
        left = jnp.concatenate([part[i] for i in range(2) for part in parts[:2]], axis=0)
        total = total + nt(left, jnp.concatenate([part[i] for i in range(2) for part in parts], axis=0))
    total = total[: 2 * SIDES] + total[2 * SIDES :]
    turned = total.T
    total = (turned[: 3 * SIDES] + turned[3 * SIDES :]).T
    gram[...] = total


def far_second(far_mid, far_top, perm, pools, interps, mid_tiles, top_tiles, right, image, near):
    return pl.pallas_call(
        far_second_kernel,
        out_shape=[
            jax.ShapeDtypeStruct((LEAVES, SIDES, LEAF), f32),
            jax.ShapeDtypeStruct((2 * SIDES, 3 * SIDES), f32),
        ],
        in_specs=[SM] * 3 + [pl.BlockSpec(memory_space=pl.ANY)] * 4 + [VM] * 11,
        out_specs=[VM] * 2,
        scratch_shapes=[
            pltpu.VMEM((4, PAY2_ROWS, LANES), bf16),
            pltpu.VMEM((16, S_ROWS, LANES), bf16),
            pltpu.VMEM((LEAVES, SIDES, RANK), bf16),
            pltpu.SemaphoreType.DMA((4,)),
        ],
        compiler_params=params(14),
        cost_estimate=lasting(8),
    )(far_mid, far_top, perm, *pools, *interps, mid_tiles, top_tiles, right, image, *near)


PARTS = 2
PART = SPAN // PARTS


def put_back(group, order, perm, image, second, rows):
    def kernel(order_ref, perm_ref, q_ref, p_ref, *refs):
        out, tree = refs[-2:]
        for member in range(LIST):
            place = LIST * group + member
            stacked = jnp.concatenate([q_ref[place], p_ref[place], jnp.zeros((2 * SIDES, LEAF), f32)], axis=0)
            tree[member * LEAF : (member + 1) * LEAF, :] = stacked.T

        for member in range(LIST):
            base = perm_ref[LIST * group + member] * LEAF

            def put(step, _, member=member, base=base):
                at = step * 64
                for u in range(64):
                    out[pl.ds(order_ref[base + at + u], 1), :] = tree[pl.ds(member * LEAF + at + u, 1), :]
                return 0

            lax.fori_loop(0, LEAF // 64, put, 0)

    earlier = [] if rows is None else [rows]
    return pl.pallas_call(
        kernel, out_shape=jax.ShapeDtypeStruct((SPAN, LANES), f32),
        in_specs=[SM] * 2 + [VM] * (2 + len(earlier)), out_specs=VM,
        scratch_shapes=[pltpu.VMEM((LIST * LEAF, LANES), f32)],
        input_output_aliases={4: 0} if earlier else {},
        compiler_params=params(12), cost_estimate=lasting(2.5),
    )(order, perm, image, second, *earlier)


def to_columns(part, rows):
    def kernel(rows_ref, out):
        for i in range(PART // LEAF):
            at = part * PART + i * LEAF
            out[:, i * LEAF : (i + 1) * LEAF] = rows_ref[at : at + LEAF, :].T[: 2 * SIDES, :]

    return pl.pallas_call(
        kernel, out_shape=jax.ShapeDtypeStruct((2 * SIDES, PART), f32), in_specs=[VM], out_specs=VM,
        compiler_params=params(12), cost_estimate=lasting(2),
    )(rows)


def dot(left, right, contract=(1, 0)):
    return lax.dot_general(
        left, right, (((contract[0],), (contract[1],)), ((), ())), preferred_element_type=f32, precision=HIGHEST
    )


def eliminate(systems):
    row = lax.broadcasted_iota(jnp.int32, (SIDES, 1), 0)
    for k in range(SIDES):
        following = []
        for matrix, values in systems:
            scale = 1.0 / matrix[k : k + 1, k : k + 1]
            column = matrix[:, k : k + 1]
            matrix_row = matrix[k : k + 1, :] * scale
            values_row = values[k : k + 1, :] * scale
            following.append((
                jnp.where(row == k, matrix_row, matrix - column * matrix_row),
                jnp.where(row == k, values_row, values - column * values_row),
            ))
        systems = following
    return [values for _, values in systems]


def finish_kernel(gram, rhs, mapped0, mapped1, x_hbm, r_hbm, x_out, r_out, sems):
    n = SIDES
    rr, rq, rp = gram[0:n, 0:n], gram[0:n, n : 2 * n], gram[0:n, 2 * n : 3 * n]
    qr, qq, qp = gram[n : 2 * n, 0:n], gram[n : 2 * n, n : 2 * n], gram[n : 2 * n, 2 * n : 3 * n]
    eye = (lax.broadcasted_iota(jnp.int32, (n, n), 0) == lax.broadcasted_iota(jnp.int32, (n, n), 1)).astype(f32)
    alpha, rr_inverse = eliminate([(0.5 * (rq + qr), rr), (rr, eye)])
    by_alpha = dot(jnp.concatenate([rq, qq, rp, qp], axis=0), alpha)
    rho = rr - by_alpha[:n] + dot(alpha, by_alpha[n : 2 * n] - qr, (0, 0))
    first = eye + dot(rr_inverse, rho)
    by_first = dot(jnp.concatenate([rq, qq], axis=0), first)
    upper, lower = by_first[:n] - by_alpha[2 * n : 3 * n], by_first[n:] - by_alpha[3 * n :]
    half = dot(first, upper, (0, 0)) - dot(alpha, lower, (0, 0))
    turned = dot(upper, first, (0, 0)) - dot(lower, alpha, (0, 0))
    (beta,) = eliminate([(0.5 * (half + turned), rho)])
    c0 = alpha + dot(first, beta)
    c1 = -dot(alpha, beta)

    lane = lax.broadcasted_iota(jnp.int32, (n, LANES), 1)
    place = lax.broadcasted_iota(jnp.int32, (n, LANES), 0)
    to_x = ((lane & 63) == place).astype(f32)
    to_r = ((lane & 63) == place + n).astype(f32)
    combine = jnp.concatenate(
        [dot(c0, to_x), dot(c1, to_x) - dot(c0, to_r), -dot(c1, to_r), jnp.zeros((n, LANES), f32)], axis=0
    ).T
    high, low = split(combine)
    upper = lax.broadcasted_iota(jnp.int32, (LANES, LANES), 0) < 2 * n
    both = jnp.where(upper, high.astype(f32), low.astype(f32)).astype(bf16)
    both = jnp.concatenate([both, both], axis=1)

    copies = []
    for i in range(LEAVES):
        span = slice(i * LEAF, (i + 1) * LEAF)
        part = (mapped0, mapped1)[i * LEAF // PART]
        at = i * LEAF % PART
        right = rhs[:, span]
        stacked = jnp.concatenate([right, part[:, at : at + LEAF], jnp.zeros((n, LEAF), f32)], axis=0)
        result = nn(both, jnp.concatenate(split(stacked), axis=0))
        result = result[: 2 * n] + result[2 * n :]
        x_out[:, span] = result[:n]
        r_out[:, span] = right + result[n:]
        if i % 4 == 3:
            done = slice((i - 3) * LEAF, (i + 1) * LEAF)
            for which, (source, target) in enumerate(((x_out, x_hbm), (r_out, r_hbm))):
                copies.append(pltpu.make_async_copy(source.at[:, done], target.at[:, done], sems.at[which, i // 4]))
                copies[-1].start()
    for copy in copies:
        copy.wait()


def finish(gram, rhs, mapped):
    return pl.pallas_call(
        finish_kernel,
        out_shape=[jax.ShapeDtypeStruct((SIDES, SPAN), f32)] * 2,
        in_specs=[VM] * 4,
        out_specs=[HBM] * 2,
        scratch_shapes=[pltpu.VMEM((SIDES, SPAN), f32)] * 2 + [pltpu.SemaphoreType.DMA((2, 4))],
        compiler_params=params(24),
    )(gram, rhs, *mapped)


def swapped(value, mask):
    count = lax.axis_size(AXES)
    return lax.ppermute(value, AXES, [(source, source ^ mask) for source in range(count)])


def gather_pools(payload, top_at, inputs, steps):
    done = []

    def beside(step, values):
        nonlocal inputs
        arrived, results, inputs = lax.optimization_barrier((values, steps[step](inputs), inputs))
        done.append(results)
        return arrived

    pair = jnp.stack([payload, beside(0, swapped(payload, 2))])
    two = pair[:, top_at:]
    four = jnp.concatenate([two, beside(1, swapped(two, 6))])
    eight = jnp.concatenate([four, beside(2, swapped(four, 8))])
    other_pair, other_eight = beside(3, (swapped(pair, 1), swapped(eight, 1)))
    return (pair, other_pair, eight, other_eight), [result for results in done for result in results]


def shards(
    points, tree_order, rhs, leaf_skel, skel_mid, skel_top, near_lists, far_mid, far_top,
    leaf_interp, interp_mid, interp_top,
):
    interps = (leaf_interp, interp_mid, interp_top)
    a_rows, b_rows, right, payload, perm = setup(
        leaf_skel, skel_mid, near_lists.T, tree_order, skel_top, points, rhs, interps
    )
    def first(*groups):
        return lambda inputs: [near_first(group, *inputs) for group in groups]

    pools, found = gather_pools(payload, MID_ROWS, (a_rows, b_rows, right), [first(0, 1), first(2), first(3), first()])
    near, tiles = zip(*found)
    lists = (far_mid, far_top.T)
    image, payload, mid_tiles, top_tiles = far_first(*lists, perm, pools, interps, right, near)
    def again(*groups):
        return lambda inputs: [near_second(group, tiles[group], *inputs) for group in groups]

    pools, near = gather_pools(payload, S1_ROWS, (image,), [again(0), again(1), again(2), again(3)])
    second, gram = far_second(*lists, perm, pools, interps, mid_tiles, top_tiles, right, image, near)
    rows = None
    for group in range(GROUPS):
        rows = put_back(group, tree_order, perm, image, second, rows)
    mapped = [to_columns(part, rows) for part in range(PARTS)]
    for mask in (1, 2, 6, 8, 24, 32, 96):
        gram = gram + swapped(gram, mask)
    return tuple(finish(gram, rhs, mapped))


def solution(mesh):
    placed = (
        P(None, AXES), P(AXES), P(None, AXES), P(AXES, None), P(AXES, None), P(), P(AXES, None), P(AXES, None), P(),
        P(AXES, None, None), P(AXES, None, None), P(AXES, None, None),
    )
    return jax.shard_map(
        shards, mesh=mesh, in_specs=placed, out_specs=(P(None, AXES), P(None, AXES)), check_vma=False
    )
```

```python
import math

import jax
import jax.numpy as jnp
from jax import lax
from jax.experimental import pallas as pl
from jax.experimental.pallas import tpu as pltpu
from jax.sharding import PartitionSpec as P

AXES = ("outer", "inner")
f32 = jnp.float32
bf16 = jnp.bfloat16
HIGHEST = lax.Precision.HIGHEST

DIM = 64
LEAVES = 16
LEAF = 512
SPAN = LEAVES * LEAF
RANK = 256
SIDES = 32
MID = 4
LIST = 4
LANES = 128
SQ = DIM
RHS_LANE = LANES - SIDES
EXPO = -(2.0 / DIM) * math.log2(math.e)
NEAR_SCALE = 32.0 / math.sqrt(LEAF * LIST)
FAR_SCALE = 64.0 / math.sqrt(RANK * LIST)

C_ROWS = RANK // 2 + 2 * 16
S_ROWS = 2 * SIDES
S1_AT = MID * C_ROWS
MID_ROWS = MID * (C_ROWS + S_ROWS)
S2_AT = MID_ROWS + C_ROWS
PAY_ROWS = S2_AT + S_ROWS
TOP_ROWS = C_ROWS + S_ROWS
S1_ROWS = MID * S_ROWS
PAY2_ROWS = S1_ROWS + S_ROWS
GROUPS = LEAVES // LIST
SKEL_MID_AT = LEAVES * RANK
PAIRS = [(p, q) for p in range(LIST) for q in range(p, LIST)]

VM = pl.BlockSpec(memory_space=pltpu.VMEM)
SM = pl.BlockSpec(memory_space=pltpu.SMEM)
HBM = pl.BlockSpec(memory_space=pltpu.HBM)


def params(mib):
    return pltpu.CompilerParams(vmem_limit_bytes=mib * 2**20)


def in_hbm(*arrays):
    return [pltpu.with_memory_space_constraint(array, pltpu.HBM) for array in arrays]


def lasting(microseconds):
    return pl.CostEstimate(flops=int(1.15e9 * microseconds), bytes_accessed=0, transcendentals=0)


def nt(left, right):
    return lax.dot_general(left, right, (((1,), (1,)), ((), ())), preferred_element_type=f32)


def nn(left, right):
    return jnp.dot(left, right, preferred_element_type=f32)


def target_side(rows):
    lane = lax.broadcasted_iota(jnp.int32, rows.shape, 1)
    values = rows.astype(f32)
    shifted = pltpu.roll(values, 3, 1)
    other = jnp.where(lane < SQ + 3, 1.0, jnp.where(lane < SQ + 6, shifted, 0.0))
    return jnp.where(lane < SQ, -2.0 * values, other).astype(bf16)


def tile(source_rows, target_rows):
    return jnp.exp2(EXPO * nt(source_rows, target_rows)).astype(bf16)


def split(values):
    high = values.astype(bf16)
    return high, (values - high.astype(f32)).astype(bf16)


def halves(pay_ref, at, values):
    for half in range(2):
        pay_ref[at + half * SIDES : at + (half + 1) * SIDES, :] = values[:, half * LANES : (half + 1) * LANES]


def joined(ref, slot, at):
    return jnp.concatenate([ref[slot, pl.ds(at + half * SIDES, SIDES), :] for half in range(2)], axis=1)


def climb(s0_ref, mid_ref, top_ref, pay_ref, s1_at, s2_at):
    total = jnp.zeros((SIDES, RANK), f32)
    for node in range(MID):
        children = jnp.concatenate([s0_ref[4 * node + k] for k in range(4)], axis=1)
        s1 = nt(children, mid_ref[node]).astype(bf16)
        halves(pay_ref, s1_at + node * S_ROWS, s1)
        total = total + nt(s1, top_ref[node])
    halves(pay_ref, s2_at, total.astype(bf16))


def pack_points(pay_ref, at, rows):
    lane = lax.broadcasted_iota(jnp.int32, (LANES, LANES), 1)
    second = pltpu.roll(rows[LANES:, :], DIM, 1)
    pay_ref[at : at + LANES, :] = jnp.where(lane < DIM, rows[:LANES, :], second).astype(bf16)
    squares = rows.T[SQ : SQ + 16, :].astype(bf16)
    for half in range(2):
        start = at + LANES + 16 * half
        pay_ref[start : start + 16, :] = squares[:, half * LANES : (half + 1) * LANES]


def unpack_points(ref, slot, at):
    lane = lax.broadcasted_iota(jnp.int32, (LANES, LANES), 1)
    packed = ref[slot, pl.ds(at, LANES), :].astype(f32)
    points = jnp.concatenate([packed, pltpu.roll(packed, DIM, 1)], axis=0)
    lane = lax.broadcasted_iota(jnp.int32, (RANK, LANES), 1)
    points = jnp.where(lane < DIM, points, jnp.where(lane < DIM + 3, 1.0, 0.0)).astype(bf16)
    squares = jnp.concatenate([ref[slot, pl.ds(at + LANES + 16 * half, 16), :] for half in range(2)], axis=1).astype(f32)
    return points, squares[0:1] + squares[1:2] + squares[2:3]


def far_tile(target, source):
    points, squares = source
    return jnp.exp2(EXPO * (nt(target, points) + squares)).astype(bf16)


def far_target(points, squares):
    lane = lax.broadcasted_iota(jnp.int32, (RANK, LANES), 1)
    values = points.astype(f32)
    columns = jnp.concatenate([squares, jnp.zeros((7, RANK), f32)], axis=0).T
    column = columns[:, 0:1]
    high = column.astype(bf16).astype(f32)
    middle = (column - high).astype(bf16).astype(f32)
    low = column - high - middle
    parts = jnp.where(lane == SQ, high, jnp.where(lane == SQ + 1, middle, jnp.where(lane == SQ + 2, low, 0.0)))
    return jnp.where(lane < SQ, -2.0 * values, parts).astype(bf16)


def setup_kernel(
    leaf_skel_hbm, skel_mid_hbm, near_hbm, order_hbm, skel_top_hbm, points_hbm, rhs_hbm, leaf_hbm, mid_hbm, top_hbm,
    a_out, b_out, r_out, pay, perm,
    lists, near, order, skel_top, points, rhs, rows, tree, skel, leaf_v, mid_v, top_v, s0, sources, sems,
):
    device = this_device()
    eight = pl.multiple_of(device // 8 * 8, 8)
    quarter = SPAN // 4
    small = [
        pltpu.make_async_copy(order_hbm, order, sems.at[0]),
        pltpu.make_async_copy(skel_top_hbm.at[pl.ds(eight, 8), :], skel_top, sems.at[1]),
    ]
    chunks = []
    for i in range(4):
        part = pl.ds(i * quarter, quarter)
        chunks.append([
            pltpu.make_async_copy(points_hbm.at[:, part], points.at[:, part], sems.at[2 + i]),
            pltpu.make_async_copy(rhs_hbm.at[:, part], rhs.at[:, part], sems.at[6 + i]),
        ])
    large = [
        pltpu.make_async_copy(leaf_hbm, leaf_v, sems.at[10]),
        pltpu.make_async_copy(mid_hbm, mid_v, sems.at[11]),
        pltpu.make_async_copy(top_hbm, top_v, sems.at[12]),
    ]
    small.append(pltpu.make_async_copy(near_hbm, near, sems.at[13]))
    for i in range(LEAVES):
        small.append(pltpu.make_async_copy(leaf_skel_hbm.at[i], lists.at[pl.ds(i * RANK, RANK)], sems.at[14 + i]))
    for i in range(MID):
        part = lists.at[pl.ds(SKEL_MID_AT + i * RANK, RANK)]
        small.append(pltpu.make_async_copy(skel_mid_hbm.at[i], part, sems.at[14 + LEAVES + i]))
    for copy in sum(chunks, []) + small:
        copy.start()

    def turn(step, _):
        at = pl.multiple_of(step * LEAF, LEAF)
        values = points[:, pl.ds(at, LEAF)].astype(f32)
        square = jnp.sum(values * values, axis=0, keepdims=True)
        high = square.astype(bf16).astype(f32)
        middle = (square - high).astype(bf16).astype(f32)
        low = square - high - middle
        row = lax.broadcasted_iota(jnp.int32, (SIDES, LEAF), 0)
        extra = jnp.where(row == 0, high, jnp.where(row == 1, middle, jnp.where(row == 2, low, jnp.where(row < 6, 1.0, 0.0))))
        stacked = jnp.concatenate([values, extra, rhs[:, pl.ds(at, LEAF)]], axis=0)
        rows[pl.ds(at, LEAF), :] = stacked.T
        return 0

    for i in range(4):
        for copy in chunks[i]:
            copy.wait()
        lax.fori_loop(4 * i, 4 * i + 4, turn, 0)
    for copy in large:
        copy.start()
    for copy in small:
        copy.wait()

    count = jnp.int32(0)
    for leaf in range(LEAVES):
        members = [near[m, leaf] & (LEAVES - 1) for m in range(LIST)]
        first = jnp.minimum(jnp.minimum(members[0], members[1]), jnp.minimum(members[2], members[3]))
        leads = first == leaf

        @pl.when(leads)
        def _(members=members, count=count):
            for m in range(LIST):
                perm[count * LIST + m] = members[m]

        count = count + leads.astype(jnp.int32)

    unroll = 32

    def pick_mid(step, _):
        base = step * unroll
        first = (base >> 8) * (4 * RANK)
        spots = [first + lists[SKEL_MID_AT + base + u] for u in range(unroll)]
        found = [order[((at >> 8) << 9) + lists[at]] for at in spots]
        for u in range(unroll):
            skel[pl.ds(base + u, 1), :] = rows[pl.ds(found[u], 1), :]
        for u in range(unroll):
            sources[base + u] = found[u]
        return 0

    lax.fori_loop(0, MID * RANK // unroll, pick_mid, 0)

    own = device & 7

    def pick_top(step, _):
        base = step * unroll
        spots = [skel_top[own, base + u] for u in range(unroll)]
        found = [sources[at] for at in spots]
        for u in range(unroll):
            skel[pl.ds(MID * RANK + base + u, 1), :] = rows[pl.ds(found[u], 1), :]
        return 0

    lax.fori_loop(0, RANK // unroll, pick_top, 0)
    for node in range(MID + 1):
        pack_points(pay, MID_ROWS if node == MID else node * C_ROWS, skel[node * RANK : (node + 1) * RANK, :])


    for copy in large:
        copy.wait()

    def one_leaf(place, _):
        leaf = perm[place]
        base = leaf * LEAF

        def pick(step, _):
            at = step * 64
            for u in range(64):
                tree[pl.ds(at + u, 1), :] = rows[pl.ds(order[base + at + u], 1), :]
            return 0

        lax.fori_loop(0, LEAF // 64, pick, 0)
        values = tree[...]
        a_out[place] = values.astype(bf16)
        b_out[place] = target_side(values)
        right = values.T[RHS_LANE:, :]
        r_out[place] = right
        s0[leaf] = nt(right.astype(bf16), leaf_v[leaf]).astype(bf16)
        return 0

    lax.fori_loop(0, LEAVES, one_leaf, 0)
    climb(s0, mid_v, top_v, pay, S1_AT, S2_AT)


def interp_scratch():
    return [
        pltpu.VMEM((LEAVES, RANK, LEAF), bf16),
        pltpu.VMEM((MID, RANK, 4 * RANK), bf16),
        pltpu.VMEM((MID, RANK, RANK), bf16),
    ]


def setup(leaf_skel, skel_mid, near, order, skel_top, points, rhs, interps):
    leaf_skel, skel_mid, near, order, skel_top, points, rhs, *interps = in_hbm(
        leaf_skel, skel_mid, near, order, skel_top, points, rhs, *interps
    )
    return pl.pallas_call(
        setup_kernel,
        out_shape=[
            jax.ShapeDtypeStruct((LEAVES, LEAF, LANES), bf16),
            jax.ShapeDtypeStruct((LEAVES, LEAF, LANES), bf16),
            jax.ShapeDtypeStruct((LEAVES, SIDES, LEAF), f32),
            jax.ShapeDtypeStruct((PAY_ROWS, LANES), bf16),
            jax.ShapeDtypeStruct((LEAVES,), jnp.int32),
        ],
        in_specs=[HBM] * 10,
        out_specs=[VM] * 4 + [SM],
        scratch_shapes=[
            pltpu.SMEM(((LEAVES + MID) * RANK,), jnp.int32),
            pltpu.SMEM((LIST, LEAVES), jnp.int32),
            pltpu.SMEM((SPAN,), jnp.int32),
            pltpu.SMEM((8, RANK), jnp.int32),
            pltpu.VMEM((DIM, SPAN), bf16),
            pltpu.VMEM((SIDES, SPAN), f32),
            pltpu.VMEM((SPAN, LANES), f32),
            pltpu.VMEM((LEAF, LANES), f32),
            pltpu.VMEM(((MID + 1) * RANK, LANES), f32),
            *interp_scratch(),
            pltpu.VMEM((LEAVES, SIDES, RANK), bf16),
            pltpu.SMEM((MID * RANK,), jnp.int32),
            pltpu.SemaphoreType.DMA((14 + LEAVES + MID,)),
        ],
        compiler_params=params(32),
        cost_estimate=lasting(20),
    )(leaf_skel, skel_mid, near, order, skel_top, points, rhs, *interps)


def apply_near(weights, tiles, out):
    for target in range(LIST):
        total = jnp.zeros((weights[0].shape[0], LEAF), f32)
        for source in range(LIST):
            block = tiles[PAIRS.index((min(source, target), max(source, target)))]
            total = total + (nn if source <= target else nt)(weights[source], block)
        out[target] = total if total.shape[0] == SIDES else total[:SIDES] + total[SIDES:]


def near_first(group, a_rows, b_rows, right):
    def kernel(a_ref, b_ref, r_ref, out, tiles):
        for i, (p, q) in enumerate(PAIRS):
            tiles[i] = tile(a_ref[LIST * group + p], b_ref[LIST * group + q])
        apply_near([r_ref[LIST * group + s].astype(bf16) for s in range(LIST)], tiles, out)

    return pl.pallas_call(
        kernel,
        out_shape=[
            jax.ShapeDtypeStruct((LIST, SIDES, LEAF), f32),
            jax.ShapeDtypeStruct((len(PAIRS), LEAF, LEAF), bf16),
        ],
        in_specs=[VM] * 3,
        out_specs=[VM] * 2,
        compiler_params=params(16),
        cost_estimate=lasting(3.3),
    )(a_rows, b_rows, right)


def near_second(group, tiles, image):
    def kernel(tiles_ref, q_ref, out):
        weights = [jnp.concatenate(split(q_ref[LIST * group + s]), axis=0) for s in range(LIST)]
        apply_near(weights, tiles_ref, out)

    return pl.pallas_call(
        kernel,
        out_shape=jax.ShapeDtypeStruct((LIST, SIDES, LEAF), f32),
        in_specs=[VM] * 2,
        out_specs=VM,
        compiler_params=params(16),
        cost_estimate=lasting(2.6),
    )(tiles, image)


def descend(mid_far, top_far, perm, mid_v, top_v, leaf_v, u0, base_ref, near_refs, out):
    u2 = (FAR_SCALE * top_far).astype(bf16)
    for node in range(MID):
        u1 = (FAR_SCALE * mid_far[node] + nn(u2, top_v[node])).astype(bf16)
        down = nn(u1, mid_v[node]).astype(bf16)
        for k in range(4):
            u0[4 * node + k] = down[:, k * RANK : (k + 1) * RANK]
    for place in range(LEAVES):
        leaf = perm[place]
        far = nn(u0[leaf], leaf_v[leaf])
        out[place] = base_ref[place] + NEAR_SCALE * near_refs[place // LIST][place % LIST] + far


def top_slot(entry, device):
    mask = (entry ^ device) & 15
    ring = ((mask >> 1) & 1) ^ ((mask >> 2) & 1)
    return ring | (((mask >> 2) & 1) << 1) | (((mask >> 3) & 1) << 2) | ((mask & 1) << 3)


def mid_slot(entry, device):
    mask = ((entry >> 2) ^ device) & 3
    return (mask >> 1) | ((mask & 1) << 1)


def this_device():
    return lax.axis_index("outer") * lax.axis_size("inner") + lax.axis_index("inner")


def mid_weights(pairs, entry, device, first):
    slot = mid_slot(entry, device)
    at = pl.multiple_of(first + (entry & 3) * S_ROWS, S_ROWS)
    return slot, joined(pairs, slot, at)


def mid_first(far_mid, pair_a, pair_b):
    def kernel(lists, near_pair, far_pair, sums, tiles, four):
        four[0:2] = near_pair[...]
        four[2:4] = far_pair[...]
        device = this_device()
        for node in range(MID):
            target = far_target(*unpack_points(four, 0, node * C_ROWS))
            total = jnp.zeros((SIDES, RANK), f32)
            for m in range(LIST):
                entry = lists[node, m]
                slot, weights = mid_weights(four, entry, device, S1_AT)
                source = unpack_points(four, slot, pl.multiple_of((entry & 3) * C_ROWS, C_ROWS))
                block = far_tile(target, source)
                tiles[node * LIST + m] = block
                total = total + nt(weights, block)
            sums[node] = total

    return pl.pallas_call(
        kernel,
        out_shape=[
            jax.ShapeDtypeStruct((MID, SIDES, RANK), f32),
            jax.ShapeDtypeStruct((MID * LIST, RANK, RANK), bf16),
        ],
        in_specs=[SM] + [VM] * 2, out_specs=[VM] * 2,
        scratch_shapes=[pltpu.VMEM((4, PAY_ROWS, LANES), bf16)],
        compiler_params=params(12), cost_estimate=lasting(3),
    )(far_mid, pair_a, pair_b)


def mid_second(far_mid, pair_a, pair_b, tiles):
    def kernel(lists, near_pair, far_pair, tiles_ref, sums, four):
        four[0:2] = near_pair[...]
        four[2:4] = far_pair[...]
        device = this_device()
        for node in range(MID):
            total = jnp.zeros((SIDES, RANK), f32)
            for m in range(LIST):
                _, weights = mid_weights(four, lists[node, m], device, 0)
                total = total + nt(weights, tiles_ref[node * LIST + m])
            sums[node] = total

    return pl.pallas_call(
        kernel, out_shape=jax.ShapeDtypeStruct((MID, SIDES, RANK), f32),
        in_specs=[SM] + [VM] * 3, out_specs=VM,
        scratch_shapes=[pltpu.VMEM((4, PAY2_ROWS, LANES), bf16)],
        compiler_params=params(12), cost_estimate=lasting(1),
    )(far_mid, pair_a, pair_b, tiles)


def products(lefts, rights):
    wide = len(rights) * SIDES
    total = jnp.zeros((2 * len(lefts) * SIDES, 2 * wide), f32)
    for place in range(LEAVES):
        parts = [[split(ref[place]) for ref in refs] for refs in (lefts, rights)]
        left, right = [jnp.concatenate([part[i] for i in range(2) for part in side], axis=0) for side in parts]
        total = total + nt(left, right)
    return total[: len(lefts) * SIDES] + total[len(lefts) * SIDES :]


def early_products(right, image):
    def kernel(r_ref, q_ref, out):
        out[...] = products((r_ref, q_ref), (r_ref, q_ref))

    return pl.pallas_call(
        kernel, out_shape=jax.ShapeDtypeStruct((2 * SIDES, LANES), f32), in_specs=[VM] * 2, out_specs=VM,
        compiler_params=params(12), cost_estimate=lasting(1),
    )(right, image)


def far_first_kernel(
    far_top, perm, eight_a, eight_b, leaf_v, mid_v, top_v, mid_far, right, near0, near1, near2, near3,
    q_out, pay, top_tiles,
    sixteen, s0,
):
    sixteen[0:8] = eight_a[...]
    sixteen[8:16] = eight_b[...]
    device = this_device()
    target = far_target(*unpack_points(sixteen, 0, 0))
    top_far = jnp.zeros((SIDES, RANK), f32)
    for m in range(LIST):
        slot = top_slot(far_top[m, device], device)
        block = far_tile(target, unpack_points(sixteen, slot, 0))
        top_tiles[m] = block
        top_far = top_far + nt(joined(sixteen, slot, C_ROWS), block)
    descend(mid_far, top_far, perm, mid_v, top_v, leaf_v, s0, right, (near0, near1, near2, near3), q_out)
    for place in range(LEAVES):
        leaf = perm[place]
        raised = nt(jnp.concatenate(split(q_out[place]), axis=0), leaf_v[leaf])
        s0[leaf] = (raised[:SIDES] + raised[SIDES:]).astype(bf16)
    climb(s0, mid_v, top_v, pay, 0, S1_ROWS)


def far_first(far_top, perm, eights, interps, mid_far, right, near):
    return pl.pallas_call(
        far_first_kernel,
        out_shape=[
            jax.ShapeDtypeStruct((LEAVES, SIDES, LEAF), f32),
            jax.ShapeDtypeStruct((PAY2_ROWS, LANES), bf16),
            jax.ShapeDtypeStruct((LIST, RANK, RANK), bf16),
        ],
        in_specs=[SM] * 2 + [VM] * 11,
        out_specs=[VM] * 3,
        scratch_shapes=[
            pltpu.VMEM((16, TOP_ROWS, LANES), bf16),
            pltpu.VMEM((LEAVES, SIDES, RANK), bf16),
        ],
        compiler_params=params(14),
        cost_estimate=lasting(8),
    )(far_top, perm, *eights, *interps, mid_far, right, *near)


def far_second_kernel(
    far_top, perm, eight_a, eight_b, leaf_v, mid_v, top_v, mid_far, top_tiles, early,
    right, image, near0, near1, near2, near3,
    p_out, gram,
    sixteen, u0,
):
    sixteen[0:8] = eight_a[...]
    sixteen[8:16] = eight_b[...]
    device = this_device()
    top_far = jnp.zeros((SIDES, RANK), f32)
    for m in range(LIST):
        top_far = top_far + nt(joined(sixteen, top_slot(far_top[m, device], device), 0), top_tiles[m])
    descend(mid_far, top_far, perm, mid_v, top_v, leaf_v, u0, image, (near0, near1, near2, near3), p_out)
    late = products((right, image), (p_out,))
    late = jnp.concatenate([late, jnp.zeros((2 * SIDES, LANES - 2 * SIDES), f32)], axis=1)
    late = pltpu.roll(late + pltpu.roll(late, LANES - SIDES, 1), 2 * SIDES, 1)
    both = early[...] + pltpu.roll(early[...], 2 * SIDES, 1)
    gram[...] = jnp.where(lax.broadcasted_iota(jnp.int32, both.shape, 1) < 2 * SIDES, both, late)


def far_second(far_top, perm, eights, interps, mid_far, top_tiles, early, right, image, near):
    return pl.pallas_call(
        far_second_kernel,
        out_shape=[
            jax.ShapeDtypeStruct((LEAVES, SIDES, LEAF), f32),
            jax.ShapeDtypeStruct((2 * SIDES, LANES), f32),
        ],
        in_specs=[SM] * 2 + [VM] * 14,
        out_specs=[VM] * 2,
        scratch_shapes=[
            pltpu.VMEM((16, S_ROWS, LANES), bf16),
            pltpu.VMEM((LEAVES, SIDES, RANK), bf16),
        ],
        compiler_params=params(14),
        cost_estimate=lasting(8),
    )(far_top, perm, *eights, *interps, mid_far, top_tiles, early, right, image, *near)


PARTS = 2
PART = SPAN // PARTS


def put_back(places, order, perm, image, second, rows):
    def kernel(order_ref, perm_ref, q_ref, p_ref, *refs):
        out, tree = refs[-2:]
        for i, place in enumerate(places):
            stacked = jnp.concatenate([q_ref[place], p_ref[place], jnp.zeros((2 * SIDES, LEAF), f32)], axis=0)
            tree[i * LEAF : (i + 1) * LEAF, :] = stacked.T

        for i, place in enumerate(places):
            base = perm_ref[place] * LEAF

            def put(step, _, i=i, base=base):
                at = step * 64
                for u in range(64):
                    out[pl.ds(order_ref[base + at + u], 1), :] = tree[pl.ds(i * LEAF + at + u, 1), :]
                return 0

            lax.fori_loop(0, LEAF // 64, put, 0)

    earlier = [] if rows is None else [rows]
    return pl.pallas_call(
        kernel, out_shape=jax.ShapeDtypeStruct((SPAN, LANES), f32),
        in_specs=[SM] * 2 + [VM] * (2 + len(earlier)), out_specs=VM,
        scratch_shapes=[pltpu.VMEM((len(places) * LEAF, LANES), f32)],
        input_output_aliases={4: 0} if earlier else {},
        compiler_params=params(12), cost_estimate=lasting(2.5),
    )(order, perm, image, second, *earlier)


def to_columns(part, rows):
    def kernel(rows_ref, out):
        for i in range(PART // LEAF):
            at = part * PART + i * LEAF
            out[:, i * LEAF : (i + 1) * LEAF] = rows_ref[at : at + LEAF, :].T[: 2 * SIDES, :]

    return pl.pallas_call(
        kernel, out_shape=jax.ShapeDtypeStruct((2 * SIDES, PART), f32), in_specs=[VM], out_specs=VM,
        compiler_params=params(12), cost_estimate=lasting(2),
    )(rows)


def dot(left, right, contract=(1, 0)):
    return lax.dot_general(
        left, right, (((contract[0],), (contract[1],)), ((), ())), preferred_element_type=f32, precision=HIGHEST
    )


def eliminate(systems):
    row = lax.broadcasted_iota(jnp.int32, (SIDES, 1), 0)
    for k in range(SIDES):
        following = []
        for matrix, values in systems:
            scale = 1.0 / matrix[k : k + 1, k : k + 1]
            column = matrix[:, k : k + 1]
            matrix_row = matrix[k : k + 1, :] * scale
            values_row = values[k : k + 1, :] * scale
            following.append((
                jnp.where(row == k, matrix_row, matrix - column * matrix_row),
                jnp.where(row == k, values_row, values - column * values_row),
            ))
        systems = following
    return [values for _, values in systems]


def finish_kernel(gram, rhs, mapped0, mapped1, x_hbm, r_hbm, x_out, r_out, sems):
    n = SIDES
    rr, rq, rp = gram[0:n, 0:n], gram[0:n, n : 2 * n], gram[0:n, 2 * n : 3 * n]
    qr, qq, qp = gram[n : 2 * n, 0:n], gram[n : 2 * n, n : 2 * n], gram[n : 2 * n, 2 * n : 3 * n]
    eye = (lax.broadcasted_iota(jnp.int32, (n, n), 0) == lax.broadcasted_iota(jnp.int32, (n, n), 1)).astype(f32)
    alpha, rr_inverse = eliminate([(0.5 * (rq + qr), rr), (rr, eye)])
    by_alpha = dot(jnp.concatenate([rq, qq, rp, qp], axis=0), alpha)
    rho = rr - by_alpha[:n] + dot(alpha, by_alpha[n : 2 * n] - qr, (0, 0))
    first = eye + dot(rr_inverse, rho)
    by_first = dot(jnp.concatenate([rq, qq], axis=0), first)
    upper, lower = by_first[:n] - by_alpha[2 * n : 3 * n], by_first[n:] - by_alpha[3 * n :]
    half = dot(first, upper, (0, 0)) - dot(alpha, lower, (0, 0))
    turned = dot(upper, first, (0, 0)) - dot(lower, alpha, (0, 0))
    (beta,) = eliminate([(0.5 * (half + turned), rho)])
    c0 = alpha + dot(first, beta)
    c1 = -dot(alpha, beta)

    lane = lax.broadcasted_iota(jnp.int32, (n, LANES), 1)
    place = lax.broadcasted_iota(jnp.int32, (n, LANES), 0)
    to_x = ((lane & 63) == place).astype(f32)
    to_r = ((lane & 63) == place + n).astype(f32)
    combine = jnp.concatenate(
        [dot(c0, to_x), dot(c1, to_x) - dot(c0, to_r), -dot(c1, to_r), jnp.zeros((n, LANES), f32)], axis=0
    ).T
    high, low = split(combine)
    upper = lax.broadcasted_iota(jnp.int32, (LANES, LANES), 0) < 2 * n
    both = jnp.where(upper, high.astype(f32), low.astype(f32)).astype(bf16)
    both = jnp.concatenate([both, both], axis=1)

    copies = []
    for i in range(LEAVES):
        span = slice(i * LEAF, (i + 1) * LEAF)
        part = (mapped0, mapped1)[i * LEAF // PART]
        at = i * LEAF % PART
        right = rhs[:, span]
        stacked = jnp.concatenate([right, part[:, at : at + LEAF], jnp.zeros((n, LEAF), f32)], axis=0)
        result = nn(both, jnp.concatenate(split(stacked), axis=0))
        result = result[: 2 * n] + result[2 * n :]
        x_out[:, span] = result[:n]
        r_out[:, span] = right + result[n:]
        if i % 4 == 3:
            done = slice((i - 3) * LEAF, (i + 1) * LEAF)
            for which, (source, target) in enumerate(((x_out, x_hbm), (r_out, r_hbm))):
                copies.append(pltpu.make_async_copy(source.at[:, done], target.at[:, done], sems.at[which, i // 4]))
                copies[-1].start()
    for copy in copies:
        copy.wait()


def finish(gram, rhs, mapped):
    return pl.pallas_call(
        finish_kernel,
        out_shape=[jax.ShapeDtypeStruct((SIDES, SPAN), f32)] * 2,
        in_specs=[VM] * 4,
        out_specs=[HBM] * 2,
        scratch_shapes=[pltpu.VMEM((SIDES, SPAN), f32)] * 2 + [pltpu.SemaphoreType.DMA((2, 4))],
        compiler_params=params(24),
    )(gram, rhs, *mapped)


def swapped(value, mask):
    count = lax.axis_size(AXES)
    return lax.ppermute(value, AXES, [(source, source ^ mask) for source in range(count)])


def gather_pools(payload, top_at, inputs, steps, beside_mid):
    done = []

    def beside(values, work):
        nonlocal inputs
        arrived, results, inputs = lax.optimization_barrier((values, work(inputs), inputs))
        done.append(results)
        return arrived

    pair = jnp.stack([payload, beside(swapped(payload, 2), steps[0])])
    two = pair[:, top_at:]
    other_two, other_pair = beside((swapped(two, 6), swapped(pair, 1)), steps[1])
    four = jnp.concatenate([two, other_two])
    other_four = beside(swapped(four, 8), lambda inputs: [beside_mid(pair, other_pair), *steps[2](inputs)])
    mid = done[2].pop(0)
    eight = jnp.concatenate([four, other_four])
    other_eight = beside(swapped(eight, 1), steps[3])
    return (eight, other_eight), mid, [result for results in done for result in results]


def shards(
    points, tree_order, rhs, leaf_skel, skel_mid, skel_top, near_lists, far_mid, far_top,
    leaf_interp, interp_mid, interp_top,
):
    interps = (leaf_interp, interp_mid, interp_top)
    a_rows, b_rows, right, payload, perm = setup(
        leaf_skel, skel_mid, near_lists.T, tree_order, skel_top, points, rhs, interps
    )

    def first(*groups):
        return lambda inputs: [near_first(group, *inputs) for group in groups]

    eights, (mid_far, mid_tiles), found = gather_pools(
        payload, MID_ROWS, (a_rows, b_rows, right), [first(0, 1), first(2), first(3), first()],
        lambda *pairs: mid_first(far_mid, *pairs),
    )
    near, tiles = zip(*found)
    image, payload, top_tiles = far_first(far_top.T, perm, eights, interps, mid_far, right, near)

    def again(*groups):
        return lambda inputs: [near_second(group, tiles[group], *inputs) for group in groups]

    early = []

    def again_and_products(inputs):
        early.append(early_products(right, *inputs))
        return again(1)(inputs)

    eights, mid_far, near = gather_pools(
        payload, S1_ROWS, (image,), [again(0), again_and_products, again(2), again(3)],
        lambda *pairs: mid_second(far_mid, *pairs, mid_tiles),
    )
    second, gram = far_second(
        far_top.T, perm, eights, interps, mid_far, top_tiles, early[0], right, image, near
    )
    rows, place = None, 0
    for mask, count in ((1, 2), (2, 3), (6, 3), (8, 3), (24, 3), (32, 2)):
        places = range(place, place + count)
        rows = put_back(places, tree_order, perm, image, second, rows)
        sent, rows = lax.optimization_barrier((swapped(gram, mask), rows))
        gram, place = gram + sent, place + count
    gram = gram + swapped(gram, 96)
    return tuple(finish(gram, rhs, [to_columns(part, rows) for part in range(PARTS)]))


def solution(mesh):
    placed = (
        P(None, AXES), P(AXES), P(None, AXES), P(AXES, None), P(AXES, None), P(), P(AXES, None), P(AXES, None), P(),
        P(AXES, None, None), P(AXES, None, None), P(AXES, None, None),
    )
    return jax.shard_map(
        shards, mesh=mesh, in_specs=placed, out_specs=(P(None, AXES), P(None, AXES)), check_vma=False
    )
```

```python
import math

import jax
import jax.numpy as jnp
from jax import lax
from jax.experimental import pallas as pl
from jax.experimental.pallas import tpu as pltpu
from jax.sharding import PartitionSpec as P

AXES = ("outer", "inner")
f32 = jnp.float32
bf16 = jnp.bfloat16
HIGHEST = lax.Precision.HIGHEST

DIM = 64
LEAVES = 16
LEAF = 512
SPAN = LEAVES * LEAF
RANK = 256
SIDES = 32
MID = 4
LIST = 4
LANES = 128
SQ = DIM
RHS_LANE = LANES - SIDES
EXPO = -(2.0 / DIM) * math.log2(math.e)
NEAR_SCALE = 32.0 / math.sqrt(LEAF * LIST)
FAR_SCALE = 64.0 / math.sqrt(RANK * LIST)

C_ROWS = RANK // 2 + 2 * 16
S_ROWS = 2 * SIDES
S1_AT = MID * C_ROWS
MID_ROWS = MID * (C_ROWS + S_ROWS)
S2_AT = MID_ROWS + C_ROWS
PAY_ROWS = S2_AT + S_ROWS
TOP_ROWS = C_ROWS + S_ROWS
S1_ROWS = MID * S_ROWS
PAY2_ROWS = S1_ROWS + S_ROWS
GROUPS = LEAVES // LIST
SKEL_MID_AT = LEAVES * RANK
PAIRS = [(p, q) for p in range(LIST) for q in range(p, LIST)]

VM = pl.BlockSpec(memory_space=pltpu.VMEM)
SM = pl.BlockSpec(memory_space=pltpu.SMEM)
HBM = pl.BlockSpec(memory_space=pltpu.HBM)


def params(mib):
    return pltpu.CompilerParams(vmem_limit_bytes=mib * 2**20)


def in_hbm(*arrays):
    return [pltpu.with_memory_space_constraint(array, pltpu.HBM) for array in arrays]


def lasting(microseconds):
    return pl.CostEstimate(flops=int(1.15e9 * microseconds), bytes_accessed=0, transcendentals=0)


def nt(left, right):
    return lax.dot_general(left, right, (((1,), (1,)), ((), ())), preferred_element_type=f32)


def nn(left, right):
    return jnp.dot(left, right, preferred_element_type=f32)


def target_side(rows):
    lane = lax.broadcasted_iota(jnp.int32, rows.shape, 1)
    values = rows.astype(f32)
    shifted = pltpu.roll(values, 3, 1)
    other = jnp.where(lane < SQ + 3, 1.0, jnp.where(lane < SQ + 6, shifted, 0.0))
    return jnp.where(lane < SQ, -2.0 * values, other).astype(bf16)


def tile(source_rows, target_rows):
    return jnp.exp2(EXPO * nt(source_rows, target_rows)).astype(bf16)


def split(values):
    high = values.astype(bf16)
    return high, (values - high.astype(f32)).astype(bf16)


def halves(pay_ref, at, values):
    for half in range(2):
        pay_ref[at + half * SIDES : at + (half + 1) * SIDES, :] = values[:, half * LANES : (half + 1) * LANES]


def joined(ref, slot, at):
    return jnp.concatenate([ref[slot, pl.ds(at + half * SIDES, SIDES), :] for half in range(2)], axis=1)


def climb(s0_ref, mid_ref, top_ref, pay_ref, s1_at, s2_at):
    total = jnp.zeros((SIDES, RANK), f32)
    for node in range(MID):
        children = jnp.concatenate([s0_ref[4 * node + k] for k in range(4)], axis=1)
        s1 = nt(children, mid_ref[node]).astype(bf16)
        halves(pay_ref, s1_at + node * S_ROWS, s1)
        total = total + nt(s1, top_ref[node])
    halves(pay_ref, s2_at, total.astype(bf16))


def pack_points(pay_ref, at, rows):
    lane = lax.broadcasted_iota(jnp.int32, (LANES, LANES), 1)
    second = pltpu.roll(rows[LANES:, :], DIM, 1)
    pay_ref[at : at + LANES, :] = jnp.where(lane < DIM, rows[:LANES, :], second).astype(bf16)
    squares = rows.T[SQ : SQ + 16, :].astype(bf16)
    for half in range(2):
        start = at + LANES + 16 * half
        pay_ref[start : start + 16, :] = squares[:, half * LANES : (half + 1) * LANES]


def unpack_points(ref, slot, at):
    lane = lax.broadcasted_iota(jnp.int32, (LANES, LANES), 1)
    packed = ref[slot, pl.ds(at, LANES), :].astype(f32)
    points = jnp.concatenate([packed, pltpu.roll(packed, DIM, 1)], axis=0)
    lane = lax.broadcasted_iota(jnp.int32, (RANK, LANES), 1)
    points = jnp.where(lane < DIM, points, jnp.where(lane < DIM + 3, 1.0, 0.0)).astype(bf16)
    squares = jnp.concatenate([ref[slot, pl.ds(at + LANES + 16 * half, 16), :] for half in range(2)], axis=1).astype(f32)
    return points, squares[0:1] + squares[1:2] + squares[2:3]


def far_tile(target, source):
    points, squares = source
    return jnp.exp2(EXPO * (nt(target, points) + squares)).astype(bf16)


def far_target(points, squares):
    lane = lax.broadcasted_iota(jnp.int32, (RANK, LANES), 1)
    values = points.astype(f32)
    columns = jnp.concatenate([squares, jnp.zeros((7, RANK), f32)], axis=0).T
    column = columns[:, 0:1]
    high = column.astype(bf16).astype(f32)
    middle = (column - high).astype(bf16).astype(f32)
    low = column - high - middle
    parts = jnp.where(lane == SQ, high, jnp.where(lane == SQ + 1, middle, jnp.where(lane == SQ + 2, low, 0.0)))
    return jnp.where(lane < SQ, -2.0 * values, parts).astype(bf16)


def setup_kernel(
    leaf_skel_hbm, skel_mid_hbm, near_hbm, order_hbm, skel_top_hbm, points_hbm, rhs_hbm, leaf_hbm, mid_hbm, top_hbm,
    a_out, b_out, r_out, pay, perm,
    lists, near, order, skel_top, points, rhs, rows, tree, skel, leaf_v, mid_v, top_v, s0, sources, sems,
):
    device = this_device()
    eight = pl.multiple_of(device // 8 * 8, 8)
    quarter = SPAN // 4
    small = [
        pltpu.make_async_copy(order_hbm, order, sems.at[0]),
        pltpu.make_async_copy(skel_top_hbm.at[pl.ds(eight, 8), :], skel_top, sems.at[1]),
    ]
    chunks = []
    for i in range(4):
        part = pl.ds(i * quarter, quarter)
        chunks.append([
            pltpu.make_async_copy(points_hbm.at[:, part], points.at[:, part], sems.at[2 + i]),
            pltpu.make_async_copy(rhs_hbm.at[:, part], rhs.at[:, part], sems.at[6 + i]),
        ])
    large = [
        pltpu.make_async_copy(leaf_hbm, leaf_v, sems.at[10]),
        pltpu.make_async_copy(mid_hbm, mid_v, sems.at[11]),
        pltpu.make_async_copy(top_hbm, top_v, sems.at[12]),
    ]
    small.append(pltpu.make_async_copy(near_hbm, near, sems.at[13]))
    for i in range(LEAVES):
        small.append(pltpu.make_async_copy(leaf_skel_hbm.at[i], lists.at[pl.ds(i * RANK, RANK)], sems.at[14 + i]))
    for i in range(MID):
        part = lists.at[pl.ds(SKEL_MID_AT + i * RANK, RANK)]
        small.append(pltpu.make_async_copy(skel_mid_hbm.at[i], part, sems.at[14 + LEAVES + i]))
    for copy in sum(chunks, []) + small:
        copy.start()

    def turn(step, _):
        at = pl.multiple_of(step * LEAF, LEAF)
        values = points[:, pl.ds(at, LEAF)].astype(f32)
        square = jnp.sum(values * values, axis=0, keepdims=True)
        high = square.astype(bf16).astype(f32)
        middle = (square - high).astype(bf16).astype(f32)
        low = square - high - middle
        row = lax.broadcasted_iota(jnp.int32, (SIDES, LEAF), 0)
        extra = jnp.where(row == 0, high, jnp.where(row == 1, middle, jnp.where(row == 2, low, jnp.where(row < 6, 1.0, 0.0))))
        stacked = jnp.concatenate([values, extra, rhs[:, pl.ds(at, LEAF)]], axis=0)
        rows[pl.ds(at, LEAF), :] = stacked.T
        return 0

    for i in range(4):
        for copy in chunks[i]:
            copy.wait()
        lax.fori_loop(4 * i, 4 * i + 4, turn, 0)
    for copy in large:
        copy.start()
    for copy in small:
        copy.wait()

    count = jnp.int32(0)
    for leaf in range(LEAVES):
        members = [near[m, leaf] & (LEAVES - 1) for m in range(LIST)]
        first = jnp.minimum(jnp.minimum(members[0], members[1]), jnp.minimum(members[2], members[3]))
        leads = first == leaf

        @pl.when(leads)
        def _(members=members, count=count):
            for m in range(LIST):
                perm[count * LIST + m] = members[m]

        count = count + leads.astype(jnp.int32)

    unroll = 32

    def pick_mid(step, _):
        base = step * unroll
        first = (base >> 8) * (4 * RANK)
        spots = [first + lists[SKEL_MID_AT + base + u] for u in range(unroll)]
        found = [order[((at >> 8) << 9) + lists[at]] for at in spots]
        for u in range(unroll):
            skel[pl.ds(base + u, 1), :] = rows[pl.ds(found[u], 1), :]
        for u in range(unroll):
            sources[base + u] = found[u]
        return 0

    lax.fori_loop(0, MID * RANK // unroll, pick_mid, 0)

    own = device & 7

    def pick_top(step, _):
        base = step * unroll
        spots = [skel_top[own, base + u] for u in range(unroll)]
        found = [sources[at] for at in spots]
        for u in range(unroll):
            skel[pl.ds(MID * RANK + base + u, 1), :] = rows[pl.ds(found[u], 1), :]
        return 0

    lax.fori_loop(0, RANK // unroll, pick_top, 0)
    for node in range(MID + 1):
        pack_points(pay, MID_ROWS if node == MID else node * C_ROWS, skel[node * RANK : (node + 1) * RANK, :])


    for copy in large:
        copy.wait()

    def one_leaf(place, _):
        leaf = perm[place]
        base = leaf * LEAF

        def pick(step, _):
            at = step * 64
            for u in range(64):
                tree[pl.ds(at + u, 1), :] = rows[pl.ds(order[base + at + u], 1), :]
            return 0

        lax.fori_loop(0, LEAF // 64, pick, 0)
        values = tree[...]
        a_out[place] = values.astype(bf16)
        b_out[place] = target_side(values)
        right = values.T[RHS_LANE:, :]
        r_out[place] = right
        s0[leaf] = nt(right.astype(bf16), leaf_v[leaf]).astype(bf16)
        return 0

    lax.fori_loop(0, LEAVES, one_leaf, 0)
    climb(s0, mid_v, top_v, pay, S1_AT, S2_AT)


def interp_scratch():
    return [
        pltpu.VMEM((LEAVES, RANK, LEAF), bf16),
        pltpu.VMEM((MID, RANK, 4 * RANK), bf16),
        pltpu.VMEM((MID, RANK, RANK), bf16),
    ]


def setup(leaf_skel, skel_mid, near, order, skel_top, points, rhs, interps):
    leaf_skel, skel_mid, near, order, skel_top, points, rhs, *interps = in_hbm(
        leaf_skel, skel_mid, near, order, skel_top, points, rhs, *interps
    )
    return pl.pallas_call(
        setup_kernel,
        out_shape=[
            jax.ShapeDtypeStruct((LEAVES, LEAF, LANES), bf16),
            jax.ShapeDtypeStruct((LEAVES, LEAF, LANES), bf16),
            jax.ShapeDtypeStruct((LEAVES, SIDES, LEAF), f32),
            jax.ShapeDtypeStruct((PAY_ROWS, LANES), bf16),
            jax.ShapeDtypeStruct((LEAVES,), jnp.int32),
        ],
        in_specs=[HBM] * 10,
        out_specs=[VM] * 4 + [SM],
        scratch_shapes=[
            pltpu.SMEM(((LEAVES + MID) * RANK,), jnp.int32),
            pltpu.SMEM((LIST, LEAVES), jnp.int32),
            pltpu.SMEM((SPAN,), jnp.int32),
            pltpu.SMEM((8, RANK), jnp.int32),
            pltpu.VMEM((DIM, SPAN), bf16),
            pltpu.VMEM((SIDES, SPAN), f32),
            pltpu.VMEM((SPAN, LANES), f32),
            pltpu.VMEM((LEAF, LANES), f32),
            pltpu.VMEM(((MID + 1) * RANK, LANES), f32),
            *interp_scratch(),
            pltpu.VMEM((LEAVES, SIDES, RANK), bf16),
            pltpu.SMEM((MID * RANK,), jnp.int32),
            pltpu.SemaphoreType.DMA((14 + LEAVES + MID,)),
        ],
        compiler_params=params(32),
        cost_estimate=lasting(20),
    )(leaf_skel, skel_mid, near, order, skel_top, points, rhs, *interps)


def apply_near(weights, tiles, out):
    for target in range(LIST):
        total = jnp.zeros((weights[0].shape[0], LEAF), f32)
        for source in range(LIST):
            block = tiles[PAIRS.index((min(source, target), max(source, target)))]
            total = total + (nn if source <= target else nt)(weights[source], block)
        out[target] = total if total.shape[0] == SIDES else total[:SIDES] + total[SIDES:]


def near_first(group, a_rows, b_rows, right):
    def kernel(a_ref, b_ref, r_ref, out, tiles):
        for i, (p, q) in enumerate(PAIRS):
            tiles[i] = tile(a_ref[LIST * group + p], b_ref[LIST * group + q])
        apply_near([r_ref[LIST * group + s].astype(bf16) for s in range(LIST)], tiles, out)

    return pl.pallas_call(
        kernel,
        out_shape=[
            jax.ShapeDtypeStruct((LIST, SIDES, LEAF), f32),
            jax.ShapeDtypeStruct((len(PAIRS), LEAF, LEAF), bf16),
        ],
        in_specs=[VM] * 3,
        out_specs=[VM] * 2,
        compiler_params=params(16),
        cost_estimate=lasting(3.3),
    )(a_rows, b_rows, right)


def near_second(group, tiles, image):
    def kernel(tiles_ref, q_ref, out):
        weights = [jnp.concatenate(split(q_ref[LIST * group + s]), axis=0) for s in range(LIST)]
        apply_near(weights, tiles_ref, out)

    return pl.pallas_call(
        kernel,
        out_shape=jax.ShapeDtypeStruct((LIST, SIDES, LEAF), f32),
        in_specs=[VM] * 2,
        out_specs=VM,
        compiler_params=params(16),
        cost_estimate=lasting(2.6),
    )(tiles, image)


def descend(mid_far, top_far, perm, mid_v, top_v, leaf_v, u0, base_ref, near_refs, out):
    u2 = (FAR_SCALE * top_far).astype(bf16)
    for node in range(MID):
        u1 = (FAR_SCALE * mid_far[node] + nn(u2, top_v[node])).astype(bf16)
        down = nn(u1, mid_v[node]).astype(bf16)
        for k in range(4):
            u0[4 * node + k] = down[:, k * RANK : (k + 1) * RANK]
    for place in range(LEAVES):
        leaf = perm[place]
        far = nn(u0[leaf], leaf_v[leaf])
        out[place] = base_ref[place] + NEAR_SCALE * near_refs[place // LIST][place % LIST] + far


def top_slot(entry, device):
    mask = (entry ^ device) & 15
    ring = ((mask >> 1) & 1) ^ ((mask >> 2) & 1)
    return ring | (((mask >> 2) & 1) << 1) | (((mask >> 3) & 1) << 2) | ((mask & 1) << 3)


def mid_slot(entry, device):
    mask = ((entry >> 2) ^ device) & 3
    return (mask >> 1) | ((mask & 1) << 1)


def this_device():
    return lax.axis_index("outer") * lax.axis_size("inner") + lax.axis_index("inner")


def mid_weights(pairs, entry, device, first):
    slot = mid_slot(entry, device)
    at = pl.multiple_of(first + (entry & 3) * S_ROWS, S_ROWS)
    return slot, joined(pairs, slot, at)


def mid_first(far_mid, pair_a, pair_b):
    def kernel(lists, near_pair, far_pair, sums, tiles, four):
        four[0:2] = near_pair[...]
        four[2:4] = far_pair[...]
        device = this_device()
        for node in range(MID):
            target = far_target(*unpack_points(four, 0, node * C_ROWS))
            total = jnp.zeros((SIDES, RANK), f32)
            for m in range(LIST):
                entry = lists[node, m]
                slot, weights = mid_weights(four, entry, device, S1_AT)
                source = unpack_points(four, slot, pl.multiple_of((entry & 3) * C_ROWS, C_ROWS))
                block = far_tile(target, source)
                tiles[node * LIST + m] = block
                total = total + nt(weights, block)
            sums[node] = total

    return pl.pallas_call(
        kernel,
        out_shape=[
            jax.ShapeDtypeStruct((MID, SIDES, RANK), f32),
            jax.ShapeDtypeStruct((MID * LIST, RANK, RANK), bf16),
        ],
        in_specs=[SM] + [VM] * 2, out_specs=[VM] * 2,
        scratch_shapes=[pltpu.VMEM((4, PAY_ROWS, LANES), bf16)],
        compiler_params=params(12), cost_estimate=lasting(3),
    )(far_mid, pair_a, pair_b)


def mid_second(far_mid, pair_a, pair_b, tiles):
    def kernel(lists, near_pair, far_pair, tiles_ref, sums, four):
        four[0:2] = near_pair[...]
        four[2:4] = far_pair[...]
        device = this_device()
        for node in range(MID):
            total = jnp.zeros((SIDES, RANK), f32)
            for m in range(LIST):
                _, weights = mid_weights(four, lists[node, m], device, 0)
                total = total + nt(weights, tiles_ref[node * LIST + m])
            sums[node] = total

    return pl.pallas_call(
        kernel, out_shape=jax.ShapeDtypeStruct((MID, SIDES, RANK), f32),
        in_specs=[SM] + [VM] * 3, out_specs=VM,
        scratch_shapes=[pltpu.VMEM((4, PAY2_ROWS, LANES), bf16)],
        compiler_params=params(12), cost_estimate=lasting(1),
    )(far_mid, pair_a, pair_b, tiles)


def products(lefts, rights):
    wide = len(rights) * SIDES
    total = jnp.zeros((2 * len(lefts) * SIDES, 2 * wide), f32)
    for place in range(LEAVES):
        parts = [[split(ref[place]) for ref in refs] for refs in (lefts, rights)]
        left, right = [jnp.concatenate([part[i] for i in range(2) for part in side], axis=0) for side in parts]
        total = total + nt(left, right)
    return total[: len(lefts) * SIDES] + total[len(lefts) * SIDES :]


def early_products(right, image):
    def kernel(r_ref, q_ref, out):
        out[...] = products((r_ref, q_ref), (r_ref, q_ref))

    return pl.pallas_call(
        kernel, out_shape=jax.ShapeDtypeStruct((2 * SIDES, LANES), f32), in_specs=[VM] * 2, out_specs=VM,
        compiler_params=params(12), cost_estimate=lasting(1),
    )(right, image)


def far_first_kernel(
    far_top, perm, eight_a, eight_b, leaf_v, mid_v, top_v, mid_far, right, near0, near1, near2, near3,
    q_out, pay, top_tiles,
    sixteen, s0,
):
    sixteen[0:8] = eight_a[...]
    sixteen[8:16] = eight_b[...]
    device = this_device()
    target = far_target(*unpack_points(sixteen, 0, 0))
    top_far = jnp.zeros((SIDES, RANK), f32)
    for m in range(LIST):
        slot = top_slot(far_top[m, device], device)
        block = far_tile(target, unpack_points(sixteen, slot, 0))
        top_tiles[m] = block
        top_far = top_far + nt(joined(sixteen, slot, C_ROWS), block)
    descend(mid_far, top_far, perm, mid_v, top_v, leaf_v, s0, right, (near0, near1, near2, near3), q_out)
    for place in range(LEAVES):
        leaf = perm[place]
        raised = nt(jnp.concatenate(split(q_out[place]), axis=0), leaf_v[leaf])
        s0[leaf] = (raised[:SIDES] + raised[SIDES:]).astype(bf16)
    climb(s0, mid_v, top_v, pay, 0, S1_ROWS)


def far_first(far_top, perm, eights, interps, mid_far, right, near):
    return pl.pallas_call(
        far_first_kernel,
        out_shape=[
            jax.ShapeDtypeStruct((LEAVES, SIDES, LEAF), f32),
            jax.ShapeDtypeStruct((PAY2_ROWS, LANES), bf16),
            jax.ShapeDtypeStruct((LIST, RANK, RANK), bf16),
        ],
        in_specs=[SM] * 2 + [VM] * 11,
        out_specs=[VM] * 3,
        scratch_shapes=[
            pltpu.VMEM((16, TOP_ROWS, LANES), bf16),
            pltpu.VMEM((LEAVES, SIDES, RANK), bf16),
        ],
        compiler_params=params(14),
        cost_estimate=lasting(8),
    )(far_top, perm, *eights, *interps, mid_far, right, *near)


def far_second_kernel(
    far_top, perm, eight_a, eight_b, leaf_v, mid_v, top_v, mid_far, top_tiles, early,
    right, image, near0, near1, near2, near3,
    p_out, gram,
    sixteen, u0,
):
    sixteen[0:8] = eight_a[...]
    sixteen[8:16] = eight_b[...]
    device = this_device()
    top_far = jnp.zeros((SIDES, RANK), f32)
    for m in range(LIST):
        top_far = top_far + nt(joined(sixteen, top_slot(far_top[m, device], device), 0), top_tiles[m])
    descend(mid_far, top_far, perm, mid_v, top_v, leaf_v, u0, image, (near0, near1, near2, near3), p_out)
    late = products((right, image), (p_out,))
    late = jnp.concatenate([late, jnp.zeros((2 * SIDES, LANES - 2 * SIDES), f32)], axis=1)
    late = pltpu.roll(late + pltpu.roll(late, LANES - SIDES, 1), 2 * SIDES, 1)
    both = early[...] + pltpu.roll(early[...], 2 * SIDES, 1)
    gram[...] = jnp.where(lax.broadcasted_iota(jnp.int32, both.shape, 1) < 2 * SIDES, both, late)


def far_second(far_top, perm, eights, interps, mid_far, top_tiles, early, right, image, near):
    return pl.pallas_call(
        far_second_kernel,
        out_shape=[
            jax.ShapeDtypeStruct((LEAVES, SIDES, LEAF), f32),
            jax.ShapeDtypeStruct((2 * SIDES, LANES), f32),
        ],
        in_specs=[SM] * 2 + [VM] * 14,
        out_specs=[VM] * 2,
        scratch_shapes=[
            pltpu.VMEM((16, S_ROWS, LANES), bf16),
            pltpu.VMEM((LEAVES, SIDES, RANK), bf16),
        ],
        compiler_params=params(14),
        cost_estimate=lasting(8),
    )(far_top, perm, *eights, *interps, mid_far, top_tiles, early, right, image, *near)


PARTS = 2
PART = SPAN // PARTS


def put_back(places, order, perm, image, second, rows):
    def kernel(order_ref, perm_ref, q_ref, p_ref, *refs):
        out, tree = refs[-2:]
        for i, place in enumerate(places):
            stacked = jnp.concatenate([q_ref[place], p_ref[place], jnp.zeros((2 * SIDES, LEAF), f32)], axis=0)
            tree[i * LEAF : (i + 1) * LEAF, :] = stacked.T

        for i, place in enumerate(places):
            base = perm_ref[place] * LEAF

            def put(step, _, i=i, base=base):
                at = step * 64
                for u in range(64):
                    out[pl.ds(order_ref[base + at + u], 1), :] = tree[pl.ds(i * LEAF + at + u, 1), :]
                return 0

            lax.fori_loop(0, LEAF // 64, put, 0)

    earlier = [] if rows is None else [rows]
    return pl.pallas_call(
        kernel, out_shape=jax.ShapeDtypeStruct((SPAN, LANES), f32),
        in_specs=[SM] * 2 + [VM] * (2 + len(earlier)), out_specs=VM,
        scratch_shapes=[pltpu.VMEM((len(places) * LEAF, LANES), f32)],
        input_output_aliases={4: 0} if earlier else {},
        compiler_params=params(12), cost_estimate=lasting(2.5),
    )(order, perm, image, second, *earlier)


def to_columns(part, rows):
    def kernel(rows_ref, out):
        for i in range(PART // LEAF):
            at = part * PART + i * LEAF
            out[:, i * LEAF : (i + 1) * LEAF] = rows_ref[at : at + LEAF, :].T[: 2 * SIDES, :]

    return pl.pallas_call(
        kernel, out_shape=jax.ShapeDtypeStruct((2 * SIDES, PART), f32), in_specs=[VM], out_specs=VM,
        compiler_params=params(12), cost_estimate=lasting(2),
    )(rows)


def dot(left, right, contract=(1, 0)):
    return lax.dot_general(
        left, right, (((contract[0],), (contract[1],)), ((), ())), preferred_element_type=f32, precision=HIGHEST
    )


def eliminate(systems):
    row = lax.broadcasted_iota(jnp.int32, (SIDES, 1), 0)
    for k in range(SIDES):
        following = []
        for matrix, values in systems:
            scale = 1.0 / matrix[k : k + 1, k : k + 1]
            column = matrix[:, k : k + 1]
            matrix_row = matrix[k : k + 1, :] * scale
            values_row = values[k : k + 1, :] * scale
            following.append((
                jnp.where(row == k, matrix_row, matrix - column * matrix_row),
                jnp.where(row == k, values_row, values - column * values_row),
            ))
        systems = following
    return [values for _, values in systems]


def finish_kernel(gram, rhs, mapped0, mapped1, x_hbm, r_hbm, x_out, r_out, sems):
    n = SIDES
    rr, rq, rp = gram[0:n, 0:n], gram[0:n, n : 2 * n], gram[0:n, 2 * n : 3 * n]
    qr, qq, qp = gram[n : 2 * n, 0:n], gram[n : 2 * n, n : 2 * n], gram[n : 2 * n, 2 * n : 3 * n]
    eye = (lax.broadcasted_iota(jnp.int32, (n, n), 0) == lax.broadcasted_iota(jnp.int32, (n, n), 1)).astype(f32)
    alpha, rr_inverse = eliminate([(0.5 * (rq + qr), rr), (rr, eye)])
    by_alpha = dot(jnp.concatenate([rq, qq, rp, qp], axis=0), alpha)
    rho = rr - by_alpha[:n] + dot(alpha, by_alpha[n : 2 * n] - qr, (0, 0))
    first = eye + dot(rr_inverse, rho)
    by_first = dot(jnp.concatenate([rq, qq], axis=0), first)
    upper, lower = by_first[:n] - by_alpha[2 * n : 3 * n], by_first[n:] - by_alpha[3 * n :]
    half = dot(first, upper, (0, 0)) - dot(alpha, lower, (0, 0))
    turned = dot(upper, first, (0, 0)) - dot(lower, alpha, (0, 0))
    (beta,) = eliminate([(0.5 * (half + turned), rho)])
    c0 = alpha + dot(first, beta)
    c1 = -dot(alpha, beta)

    lane = lax.broadcasted_iota(jnp.int32, (n, LANES), 1)
    place = lax.broadcasted_iota(jnp.int32, (n, LANES), 0)
    to_x = ((lane & 63) == place).astype(f32)
    to_r = ((lane & 63) == place + n).astype(f32)
    combine = jnp.concatenate(
        [dot(c0, to_x), dot(c1, to_x) - dot(c0, to_r), -dot(c1, to_r), jnp.zeros((n, LANES), f32)], axis=0
    ).T
    high, low = split(combine)
    upper = lax.broadcasted_iota(jnp.int32, (LANES, LANES), 0) < 2 * n
    both = jnp.where(upper, high.astype(f32), low.astype(f32)).astype(bf16)
    both = jnp.concatenate([both, both], axis=1)

    copies = []
    for i in range(LEAVES):
        span = slice(i * LEAF, (i + 1) * LEAF)
        part = (mapped0, mapped1)[i * LEAF // PART]
        at = i * LEAF % PART
        right = rhs[:, span]
        stacked = jnp.concatenate([right, part[:, at : at + LEAF], jnp.zeros((n, LEAF), f32)], axis=0)
        result = nn(both, jnp.concatenate(split(stacked), axis=0))
        result = result[: 2 * n] + result[2 * n :]
        x_out[:, span] = result[:n]
        r_out[:, span] = right + result[n:]
        if i % 4 == 3:
            done = slice((i - 3) * LEAF, (i + 1) * LEAF)
            for which, (source, target) in enumerate(((x_out, x_hbm), (r_out, r_hbm))):
                copies.append(pltpu.make_async_copy(source.at[:, done], target.at[:, done], sems.at[which, i // 4]))
                copies[-1].start()
    for copy in copies:
        copy.wait()


def finish(gram, rhs, mapped):
    return pl.pallas_call(
        finish_kernel,
        out_shape=[jax.ShapeDtypeStruct((SIDES, SPAN), f32)] * 2,
        in_specs=[VM] * 4,
        out_specs=[HBM] * 2,
        scratch_shapes=[pltpu.VMEM((SIDES, SPAN), f32)] * 2 + [pltpu.SemaphoreType.DMA((2, 4))],
        compiler_params=params(24),
    )(gram, rhs, *mapped)


def swapped(value, mask):
    count = lax.axis_size(AXES)
    return lax.ppermute(value, AXES, [(source, source ^ mask) for source in range(count)])


def gather_pools(payload, top_at, inputs, steps, beside_mid):
    done = []

    def beside(values, work):
        nonlocal inputs
        arrived, results, inputs = lax.optimization_barrier((values, work(inputs), inputs))
        done.append(results)
        return arrived

    pair = jnp.stack([payload, beside(swapped(payload, 2), steps[0])])
    two = pair[:, top_at:]
    other_two, other_pair = beside((swapped(two, 6), swapped(pair, 1)), steps[1])
    four = jnp.concatenate([two, other_two])
    other_four = beside(swapped(four, 8), lambda inputs: [beside_mid(pair, other_pair), *steps[2](inputs)])
    mid = done[2].pop(0)
    eight = jnp.concatenate([four, other_four])
    other_eight = beside(swapped(eight, 1), steps[3])
    return (eight, other_eight), mid, [result for results in done for result in results]


def shards(
    points, tree_order, rhs, leaf_skel, skel_mid, skel_top, near_lists, far_mid, far_top,
    leaf_interp, interp_mid, interp_top,
):
    interps = (leaf_interp, interp_mid, interp_top)
    a_rows, b_rows, right, payload, perm = setup(
        leaf_skel, skel_mid, near_lists.T, tree_order, skel_top, points, rhs, interps
    )

    def first(*groups):
        return lambda inputs: [near_first(group, *inputs) for group in groups]

    eights, (mid_far, mid_tiles), found = gather_pools(
        payload, MID_ROWS, (a_rows, b_rows, right), [first(0, 1), first(2), first(3), first()],
        lambda *pairs: mid_first(far_mid, *pairs),
    )
    near, tiles = zip(*found)
    image, payload, top_tiles = far_first(far_top.T, perm, eights, interps, mid_far, right, near)

    def again(*groups):
        return lambda inputs: [near_second(group, tiles[group], *inputs) for group in groups]

    early = []

    def again_and_products(inputs):
        early.append(early_products(right, *inputs))
        return again(2)(inputs)

    eights, mid_far, near = gather_pools(
        payload, S1_ROWS, (image,), [again(0, 1), again_and_products, again(3), again()],
        lambda *pairs: mid_second(far_mid, *pairs, mid_tiles),
    )
    second, gram = far_second(
        far_top.T, perm, eights, interps, mid_far, top_tiles, early[0], right, image, near
    )
    rows, place = None, 0
    for mask, count in ((1, 2), (2, 3), (6, 3), (8, 3), (24, 3), (32, 2)):
        places = range(place, place + count)
        rows = put_back(places, tree_order, perm, image, second, rows)
        sent, rows = lax.optimization_barrier((swapped(gram, mask), rows))
        gram, place = gram + sent, place + count
    gram = gram + swapped(gram, 96)
    return tuple(finish(gram, rhs, [to_columns(part, rows) for part in range(PARTS)]))


def solution(mesh):
    placed = (
        P(None, AXES), P(AXES), P(None, AXES), P(AXES, None), P(AXES, None), P(), P(AXES, None), P(AXES, None), P(),
        P(AXES, None, None), P(AXES, None, None), P(AXES, None, None),
    )
    return jax.shard_map(
        shards, mesh=mesh, in_specs=placed, out_specs=(P(None, AXES), P(None, AXES)), check_vma=False
    )
```
